128 devices in a mesh: lat: 16 (over y, z_hi, core), lon: 8 (over z_lo, x).
Axes of the slice: x: 4, y: 4, z: 4 (z_hi: 2, z_lo: 2; z = z_hi * 2 + z_lo), core: 2. Of those that a mesh axis runs over, the one named last changes fastest.
Arguments:
- fields: bfloat16 [4, 128, 512, 640], P(None, 'lat', 'lon'), may hold values from -6 to 6
- kernel: float32 [128, 9, 3, 512], P('lat'), may hold values from -0.09375 to 0.09375
- theta: float32 [3, 640], P(None, 'lon'), may hold values from -4 to 4
- row_start: int32 [128], P('lat'), may hold values from 0 to 123, as said below
- row_count: int32 [128], P('lat'), may hold values from 1 to 9
- norm_gain: float32 [640], replicated, may hold values from 0.1 to 1.9
- w_in: bfloat16 [640, 1280], replicated, may hold values from -0.25 to 0.25
- b_in: float32 [1280], replicated, may hold values from -3 to 3
- w_out: bfloat16 [1280, 640], replicated, may hold values from -0.15625 to 0.15625
Outputs:
- block_out: bfloat16 [4, 128, 512, 640], P(None, 'lat', 'lon')
The draws below stay inside these ranges and needn't reach their ends.
Inputs may be any that keep to these rules, and one draw needn't show every extreme that they name: Output row i draws on rows row_start[i] to row_start[i] + row_count[i] - 1, all inside the grid and within 4 rows of i.
All inputs are finite; a program needn't handle non-finite values.
Results may differ from the reference program's by a relative error of at most 0.0085.
Values may be sent and summed in bfloat16 or wider, within the bound.
No kernel may reach another device: no remote copies, remote signals or barrier semaphores. Data moves between devices by JAX's collectives and lax.ppermute only.
A program may use at most 192 MiB of HBM per device.

```python
import jax
import jax.numpy as jnp
from jax import lax

C = 640
HID = 1280
KBASIS = 3
REACH = 4
SLOTS = 9
ENS = 4
LAT_DEV = 8
NLAT = 128
NLON = 512


def support_rows(key):
    position = jnp.arange(NLAT, dtype=jnp.int32)
    lowest = jnp.maximum(position - REACH, 0)
    highest = jnp.minimum(position + REACH + 1, NLAT)
    counts = jax.random.randint(jax.random.fold_in(key, 11), (NLAT,), 1, SLOTS + 1)
    offsets = jax.random.randint(jax.random.fold_in(key, 12), (NLAT,), 0, SLOTS)
    offsets = offsets % (SLOTS - counts + 1)
    starts = position - REACH + offsets
    polar = (position < LAT_DEV) | (position >= NLAT - LAT_DEV)
    starts = jnp.where(polar, lowest, starts)
    counts = jnp.where(polar, highest - lowest, counts)
    return (starts.astype(jnp.int32), counts.astype(jnp.int32))


def draw_row_start(key, part):
    return support_rows(key)[0]


def draw_row_count(key, part):
    return support_rows(key)[1]


def shard_levels(stream_key, dims, shards, smallest, top_value):
    def one(dim, blocks):
        steps = jax.random.uniform(jax.random.fold_in(jax.random.fold_in(stream_key, 6), dim), (blocks,), jnp.float32, smallest / len(shards), top_value / len(shards))
        return jnp.repeat(jnp.exp(steps), dims[dim] // blocks).reshape((-1,) + (1,) * (len(dims) - dim - 1))

    level = one(*shards[0])
    for cut in shards[1:]:
        level = level * one(*cut)
    return level


def centred(stream_key, dims, deviation, bound, split=(), kind=jnp.bfloat16):
    loudness = shard_levels(stream_key, dims, split, -0.22, 0.18) if split else 1.0
    entries = jax.random.normal(stream_key, dims, jnp.float32) * deviation * loudness
    return jnp.minimum(jnp.maximum(entries, -bound), bound).astype(kind)


def setup_inputs(seed: int = 0) -> dict:
    key_of = jax.random.split(jax.random.key(seed), 10)
    return {
        "fields": centred(key_of[0], (ENS, NLAT, NLON, C), 1.0, 6.0, ((1, 16), (2, 8))),
        "kernel": centred(key_of[1], (NLAT, SLOTS, KBASIS, NLON), (NLON * SLOTS) ** -0.5, 0.09375, ((0, 16),), jnp.float32),
        "theta": centred(key_of[2], (KBASIS, C), 1.0, 4.0, ((1, 8),), jnp.float32),
        "row_start": draw_row_start(jax.random.fold_in(key_of[9], 71), 0),
        "row_count": draw_row_count(jax.random.fold_in(key_of[9], 71), 0),
        "norm_gain": jnp.clip(1.0 + 0.18 * jax.random.normal(key_of[5], (C,), jnp.float32), 0.1, 1.9),
        "w_in": centred(key_of[6], (C, HID), C ** -0.5, 0.25),
        "b_in": centred(key_of[7], (HID,), 0.5, 3.0, (), jnp.float32),
        "w_out": centred(key_of[8], (HID, C), HID ** -0.5, 0.15625),
    }


def conv_member(member, kernel_hat, theta, row_start, row_count):
    spectrum = jnp.fft.fft(member.astype(jnp.float32), axis=1)
    total = jnp.zeros(spectrum.shape, spectrum.dtype)
    for slot in range(SLOTS):
        mixed = jnp.einsum('ikf,kc->ifc', kernel_hat[:, slot], theta)
        source = jnp.clip(row_start + slot, 0, NLAT - 1).astype(jnp.int32)
        live = (slot < row_count)[:, None, None]
        total = total + jnp.where(live, mixed * spectrum[source], jnp.zeros_like(total))
    return jnp.real(jnp.fft.ifft(total, axis=1)).astype(jnp.bfloat16)

def mlp_member(pair, norm_gain, w_in, b_in, w_out):
    member, conv = pair
    values = conv.astype(jnp.float32)
    mean = lax.optimization_barrier(jnp.mean(values, axis=-1, keepdims=True))
    var = lax.optimization_barrier(jnp.mean((values - mean) ** 2, axis=-1, keepdims=True))
    normed = ((values - mean) * lax.rsqrt(var + 1e-05) * norm_gain).astype(jnp.bfloat16)
    hidden = jax.nn.gelu(jnp.einsum('alc,ch->alh', normed.astype(jnp.float32), w_in.astype(jnp.float32)) + b_in, approximate=False).astype(jnp.bfloat16)
    branch = jnp.einsum('alh,hc->alc', hidden.astype(jnp.float32), w_out.astype(jnp.float32))
    return (member.astype(jnp.float32) + branch).astype(jnp.bfloat16)

def reference(fields, kernel, theta, row_start, row_count, norm_gain, w_in, b_in, w_out):
    kernel_hat = jnp.fft.fft(kernel, axis=3)
    conv = lax.map(lambda member: conv_member(member, kernel_hat, theta, row_start, row_count), fields)
    return lax.map(lambda pair: mlp_member(pair, norm_gain, w_in, b_in, w_out), (fields, conv))
```

```python
import functools

import jax
import jax.numpy as jnp
import ml_dtypes
import numpy as np
from jax import lax
from jax.experimental import pallas as pl
from jax.experimental.pallas import tpu as pltpu
from jax.sharding import PartitionSpec as P

BF16 = jnp.bfloat16
F32 = jnp.float32

LON_DEV = 8
ROWS = 8
HALF = 4
ENS = 4
CHUNK = 64
CHAN = 640
CH = 80
COLS = ENS * CH
NLON = 512
SLOTS = 9
KB = 3
FB = 16
FS = 16
WIN = 12
PTS = ENS * HALF * CHUNK
HID = 1280
VMEM = 56 * 1024 * 1024


def tables():
    point = np.arange(NLON)
    freq = np.arange(NLON // 2)
    angle = 2.0 * np.pi * ((freq[:, None] * point[None, :]) % NLON) / NLON
    re, im = np.cos(angle), -np.sin(angle)
    im[0] = np.cos(np.pi * point)
    weight = np.full((NLON // 2, 1), 2.0 / NLON)
    weight[0] = 1.0 / NLON
    onward = np.stack([re.reshape(FB, FS, NLON), im.reshape(FB, FS, NLON)], axis=1)
    back = np.stack(
        [(re * weight).reshape(FB, FS, NLON), (im * weight).reshape(FB, FS, NLON)], axis=1
    )
    return (
        onward.reshape(NLON, NLON).astype(ml_dtypes.bfloat16),
        back.reshape(NLON, NLON).astype(ml_dtypes.bfloat16),
    )


def params(*semantics):
    return pltpu.CompilerParams(vmem_limit_bytes=VMEM, dimension_semantics=semantics)


def cost(flops, nbytes):
    return pl.CostEstimate(flops=int(flops), bytes_accessed=int(nbytes), transcendentals=0)


def pack_kernel(x_ref, o_ref):
    x = x_ref[0].reshape(HALF * CHUNK, CHAN)
    o_ref[...] = x.T


def pack(fields, half):
    wide = HALF * CHUNK
    return pl.pallas_call(
        pack_kernel,
        grid=(ENS,),
        in_specs=[pl.BlockSpec((1, HALF, CHUNK, CHAN), lambda e: (e, half, 0, 0))],
        out_specs=pl.BlockSpec((CHAN, wide), lambda e: (0, e)),
        out_shape=jax.ShapeDtypeStruct((CHAN, PTS), BF16),
        compiler_params=params("arbitrary"),
        cost_estimate=cost(0, 4 * CHAN * PTS),
        name="pack",
    )(fields)


def dft_rows_kernel(x_ref, w_ref, o_ref):
    for pair in range(2):
        rows = [[], []]
        for e in range(ENS):
            parts = [[], []]
            base = (e * 2 + pair) * 128
            for d in range(LON_DEV):
                tile = x_ref[d * CH : (d + 1) * CH, base : base + 128]
                parts[0].append(tile[:, :CHUNK])
                parts[1].append(tile[:, CHUNK:])
            for r in range(2):
                rows[r].append(jnp.concatenate(parts[r], axis=1))
        for r in range(2):
            x = jnp.concatenate(rows[r], axis=0)
            s = lax.dot_general(
                w_ref[...], x, (((1,), (1,)), ((), ())), preferred_element_type=F32
            )
            at = (pair * 2 + r) * 2 * FS
            o_ref[:, at : at + 2 * FS, :] = s.astype(BF16).reshape(FB, 2 * FS, COLS)


def dft(received, onward):
    return pl.pallas_call(
        dft_rows_kernel,
        out_shape=jax.ShapeDtypeStruct((FB, HALF * 2 * FS, COLS), BF16),
        compiler_params=params(),
        cost_estimate=cost(2 * HALF * NLON * NLON * COLS, 8 * CHAN * PTS),
        name="dft",
    )(received, onward)


def coef_kernel(start_ref, count_ref, first_ref, k_ref, w_ref, o_ref):
    half = pl.program_id(0)
    kern = k_ref[...].astype(BF16)
    hat = lax.dot_general(w_ref[...], kern, (((1,), (1,)), ((), ())), preferred_element_type=F32)
    hat = hat.astype(BF16).reshape(FB, 2, FS, SLOTS * KB * HALF)
    hat_re = hat[:, 0].reshape(FB * FS, SLOTS * KB * HALF)
    hat_im = hat[:, 1].reshape(FB * FS, SLOTS * KB * HALF)
    lanes = WIN * 2 * FS
    taps = SLOTS * KB * HALF
    tap = lax.broadcasted_iota(jnp.int32, (taps, lanes), 0)
    window = lax.broadcasted_iota(jnp.int32, (taps, lanes), 1) // (2 * FS)
    lane = lax.broadcasted_iota(jnp.int32, (FB * FS, lanes), 1)
    freq = lax.broadcasted_iota(jnp.int32, (FB * FS, lanes), 0)
    same = (lane % FS) == (freq % FS)
    imag = (lane // FS) % 2 == 1
    zero = freq == 0
    for i in range(HALF):
        row = half * HALF + i
        offset = start_ref[row] - (first_ref[0] + (half - 1) * HALF)
        slot = window - offset
        live = (slot >= 0) & (slot < count_ref[row])
        for k in range(KB):
            pick = (live & (tap == (i * SLOTS + slot) * KB + k)).astype(F32).astype(BF16)
            re = jnp.dot(hat_re, pick, preferred_element_type=F32)
            im = jnp.dot(hat_im, pick, preferred_element_type=F32)
            top = jnp.where(imag, jnp.where(zero, 0.0, -im), re)
            low = jnp.where(imag, jnp.where(zero, im, re), jnp.where(zero, 0.0, im))
            top = jnp.where(same, top, 0.0).astype(BF16).reshape(FB, FS, lanes)
            low = jnp.where(same, low, 0.0).astype(BF16).reshape(FB, FS, lanes)
            at = (i * KB + k) * 2 * FS
            o_ref[0, :, at : at + FS, :] = top
            o_ref[0, :, at + FS : at + 2 * FS, :] = low


def coefs(row_start, row_count, first, kernel, onward):
    smem = pl.BlockSpec(memory_space=pltpu.SMEM)
    taps = HALF * SLOTS * KB
    size = HALF * KB * 2 * FS
    return pl.pallas_call(
        coef_kernel,
        grid=(2,),
        in_specs=[
            smem,
            smem,
            smem,
            pl.BlockSpec((None, taps, NLON), lambda h: (h, 0, 0)),
            pl.BlockSpec((NLON, NLON), lambda h: (0, 0)),
        ],
        out_specs=pl.BlockSpec((1, FB, size, WIN * 2 * FS), lambda h: (h, 0, 0, 0)),
        out_shape=jax.ShapeDtypeStruct((2, FB, size, WIN * 2 * FS), BF16),
        compiler_params=params("arbitrary"),
        cost_estimate=cost(8e9, 1e7),
        name="coefs",
    )(row_start, row_count, first, kernel.reshape(2, taps, NLON), onward)


STEP = 4


def mix_kernel(g_ref, a_ref, b_ref, c_ref, theta_ref, back_ref, o_ref, t_ref):
    step = pl.program_id(0)
    theta = [theta_ref[k : k + 1, :] for k in range(KB)]
    for f in range(STEP):
        x = jnp.concatenate([a_ref[f], b_ref[f], c_ref[f]], axis=0)
        p = jnp.dot(g_ref[0, f], x, preferred_element_type=F32)
        for i in range(HALF):
            total = None
            for k in range(KB):
                at = (i * KB + k) * 2 * FS
                term = p[at : at + 2 * FS, :] * theta[k]
                total = term if total is None else total + term
            t_ref[i, pl.ds((step * STEP + f) * 2 * FS, 2 * FS), :] = total.astype(BF16)

    @pl.when(step == FB // STEP - 1)
    def _():
        for pair in range(2):
            y = [
                lax.dot_general(
                    t_ref[pair * 2 + r],
                    back_ref[...],
                    (((0,), (0,)), ((), ())),
                    preferred_element_type=F32,
                ).astype(BF16)
                for r in range(2)
            ]
            for e in range(ENS):
                base = (e * 2 + pair) * 128
                for d in range(LON_DEV):
                    o_ref[d * CH : (d + 1) * CH, base : base + 128] = jnp.concatenate(
                        [v[e * CH : (e + 1) * CH, d * CHUNK : (d + 1) * CHUNK] for v in y], axis=1
                    )


def mix(coef, half, spectra, theta, back):
    size = HALF * KB * 2 * FS
    spec = pl.BlockSpec((STEP, HALF * 2 * FS, COLS), lambda s: (s, 0, 0))
    return pl.pallas_call(
        mix_kernel,
        grid=(FB // STEP,),
        in_specs=[
            pl.BlockSpec((1, STEP, size, WIN * 2 * FS), lambda s: (half, s, 0, 0)),
            spec,
            spec,
            spec,
            pl.BlockSpec((KB, COLS), lambda s: (0, 0)),
            pl.BlockSpec((NLON, NLON), lambda s: (0, 0)),
        ],
        out_specs=pl.BlockSpec((CHAN, PTS), lambda s: (0, 0)),
        out_shape=jax.ShapeDtypeStruct((CHAN, PTS), BF16),
        scratch_shapes=[pltpu.VMEM((HALF, NLON, COLS), BF16)],
        compiler_params=params("arbitrary"),
        cost_estimate=cost(4e9, 1.6e7),
        name="mix",
    )(coef, *spectra, theta, back)


def mlp_kernel(y_ref, x_ref, gain_ref, w_in_ref, b_in_ref, w_out_ref, *rest):
    o_ref = rest[-1]
    values = y_ref[...].astype(F32)
    mean = jnp.mean(values, axis=0, keepdims=True)
    away = values - mean
    var = jnp.mean(away * away, axis=0, keepdims=True)
    normed = (away * lax.rsqrt(var + 1e-5) * gain_ref[...]).astype(BF16)
    hidden = jnp.dot(normed.T, w_in_ref[...], preferred_element_type=F32) + b_in_ref[...]
    hidden = (0.5 * hidden * (1.0 + lax.erf(hidden * np.float32(0.5**0.5)))).astype(BF16)
    branch = jnp.dot(hidden, w_out_ref[...], preferred_element_type=F32)
    x = x_ref[0].reshape(HALF * CHUNK, CHAN).astype(F32)
    o_ref[0] = (x + branch).astype(BF16).reshape(HALF, CHUNK, CHAN)


def mlp(y, fields, half, gain, w_in, b_in, w_out, before=None):
    wide = HALF * CHUNK
    points = pl.BlockSpec((1, HALF, CHUNK, CHAN), lambda e: (e, half, 0, 0))
    whole = lambda *shape: pl.BlockSpec(shape, lambda e: (0, 0))
    extra = () if before is None else (before,)
    return pl.pallas_call(
        mlp_kernel,
        grid=(ENS,),
        in_specs=[
            pl.BlockSpec((CHAN, wide), lambda e: (0, e)),
            points,
            whole(CHAN, 1),
            whole(CHAN, HID),
            whole(1, HID),
            whole(HID, CHAN),
        ]
        + [pl.BlockSpec(memory_space=pl.ANY)] * len(extra),
        out_specs=points,
        out_shape=jax.ShapeDtypeStruct((ENS, ROWS, CHUNK, CHAN), BF16),
        input_output_aliases={6: 0} if extra else {},
        compiler_params=params("arbitrary"),
        cost_estimate=cost(4 * PTS * CHAN * HID, 1.2e7),
        name="mlp",
    )(y, fields, gain, w_in, b_in, w_out, *extra)


def shards(fields, kernel, theta, row_start, row_count, norm_gain, w_in, b_in, w_out):
    onward, back = (jnp.asarray(t) for t in tables())
    size = lax.axis_size("lat")
    up = [(i, i + 1) for i in range(size - 1)]
    down = [(j, i) for i, j in up]
    swap = functools.partial(
        lax.all_to_all, axis_name="lon", split_axis=0, concat_axis=0, tiled=True
    )
    low = swap(pack(fields, 0))
    high = swap(pack(fields, 1))
    after = lax.ppermute(low, "lat", down)
    before = lax.ppermute(high, "lat", up)
    first = (lax.axis_index("lat") * ROWS).astype(jnp.int32).reshape(1)
    coef = coefs(row_start, row_count, first, kernel, onward)
    theta4 = jnp.tile(theta, (1, ENS))
    spec_low = dft(low, onward)
    spec_high = dft(high, onward)
    spec_after = dft(after, onward)
    conv_high = swap(mix(coef, 1, (spec_low, spec_high, spec_after), theta4, back))
    spec_before = dft(before, onward)
    conv_low = swap(mix(coef, 0, (spec_before, spec_low, spec_high), theta4, back))
    rest = (norm_gain[:, None], w_in, b_in[None, :], w_out)
    out = mlp(conv_high, fields, 1, *rest)
    return mlp(conv_low, fields, 0, *rest, before=out)


def solution(mesh):
    placed = (
        P(None, "lat", "lon", None),
        P("lat", None, None, None),
        P(None, "lon"),
        P("lat"),
        P("lat"),
        P(),
        P(),
        P(),
        P(),
    )
    return jax.shard_map(
        shards, mesh=mesh, in_specs=placed, out_specs=P(None, "lat", "lon", None), check_vma=False
    )
```

```python
import functools

import jax
import jax.numpy as jnp
import ml_dtypes
import numpy as np
from jax import lax
from jax.experimental import pallas as pl
from jax.experimental.pallas import tpu as pltpu
from jax.sharding import PartitionSpec as P

BF16 = jnp.bfloat16
F32 = jnp.float32

LON_DEV = 8
ROWS = 8
HALF = 4
ENS = 4
CHUNK = 64
CHAN = 640
CH = 80
COLS = ENS * CH
NLON = 512
SLOTS = 9
KB = 3
FB = 16
FS = 16
WIN = 12
PTS = ENS * HALF * CHUNK
HID = 1280
MID = CHAN // 2
VMEM = 56 * 1024 * 1024


def tables():
    point = np.arange(NLON)
    freq = np.arange(NLON // 2)
    angle = 2.0 * np.pi * ((freq[:, None] * point[None, :]) % NLON) / NLON
    re, im = np.cos(angle), -np.sin(angle)
    im[0] = np.cos(np.pi * point)
    weight = np.full((NLON // 2, 1), 2.0 / NLON)
    weight[0] = 1.0 / NLON
    onward = np.stack([re.reshape(FB, FS, NLON), im.reshape(FB, FS, NLON)], axis=1)
    back = np.stack(
        [(re * weight).reshape(FB, FS, NLON), (im * weight).reshape(FB, FS, NLON)], axis=1
    )
    return (
        onward.reshape(NLON, NLON).astype(ml_dtypes.bfloat16),
        back.reshape(NLON, NLON).astype(ml_dtypes.bfloat16),
    )


def params(*semantics):
    return pltpu.CompilerParams(vmem_limit_bytes=VMEM, dimension_semantics=semantics)


def cost(flops, nbytes):
    return pl.CostEstimate(flops=int(flops), bytes_accessed=int(nbytes), transcendentals=0)


def pack_kernel(turn_ref, x_ref, *rest):
    o_ref = rest[-1]
    x = x_ref[0].reshape(HALF * CHUNK, CHAN).T
    at = pl.multiple_of(turn_ref[0] * MID, MID)
    o_ref[pl.ds(at, MID), :] = x[:MID]
    o_ref[pl.ds(MID - at, MID), :] = x[MID:]


def pack(turn, fields, half, *after):
    wide = HALF * CHUNK
    return pl.pallas_call(
        pack_kernel,
        grid=(ENS,),
        in_specs=[
            pl.BlockSpec(memory_space=pltpu.SMEM),
            pl.BlockSpec((1, HALF, CHUNK, CHAN), lambda e: (e, half, 0, 0)),
        ]
        + [pl.BlockSpec(memory_space=pl.ANY)] * len(after),
        out_specs=pl.BlockSpec((CHAN, wide), lambda e: (0, e)),
        out_shape=jax.ShapeDtypeStruct((CHAN, PTS), BF16),
        compiler_params=params("arbitrary"),
        cost_estimate=cost(0, 4 * CHAN * PTS),
        name="pack",
    )(turn, fields, *after)


def dft_rows_kernel(x_ref, w_ref, o_ref):
    for pair in range(2):
        rows = [[], []]
        for e in range(ENS):
            parts = [[], []]
            base = (e * 2 + pair) * 128
            for d in range(LON_DEV):
                tile = x_ref[d * CH : (d + 1) * CH, base : base + 128]
                parts[0].append(tile[:, :CHUNK])
                parts[1].append(tile[:, CHUNK:])
            for r in range(2):
                rows[r].append(jnp.concatenate(parts[r], axis=1))
        for r in range(2):
            x = jnp.concatenate(rows[r], axis=0)
            s = lax.dot_general(
                w_ref[...], x, (((1,), (1,)), ((), ())), preferred_element_type=F32
            )
            at = (pair * 2 + r) * 2 * FS
            o_ref[:, at : at + 2 * FS, :] = s.astype(BF16).reshape(FB, 2 * FS, COLS)


def dft(received, onward):
    return pl.pallas_call(
        dft_rows_kernel,
        out_shape=jax.ShapeDtypeStruct((FB, HALF * 2 * FS, COLS), BF16),
        compiler_params=params(),
        cost_estimate=cost(2 * HALF * NLON * NLON * COLS, 8 * CHAN * PTS),
        name="dft",
    )(received, onward)


def coef_kernel(start_ref, count_ref, first_ref, k_ref, w_ref, *rest):
    o_ref = rest[-1]
    half = pl.program_id(0)
    kern = k_ref[...].astype(BF16)
    hat = lax.dot_general(w_ref[...], kern, (((1,), (1,)), ((), ())), preferred_element_type=F32)
    hat = hat.astype(BF16).reshape(FB, 2, FS, SLOTS * KB * HALF)
    hat_re = hat[:, 0].reshape(FB * FS, SLOTS * KB * HALF)
    hat_im = hat[:, 1].reshape(FB * FS, SLOTS * KB * HALF)
    lanes = WIN * 2 * FS
    taps = SLOTS * KB * HALF
    tap = lax.broadcasted_iota(jnp.int32, (taps, lanes), 0)
    window = lax.broadcasted_iota(jnp.int32, (taps, lanes), 1) // (2 * FS)
    lane = lax.broadcasted_iota(jnp.int32, (FB * FS, lanes), 1)
    freq = lax.broadcasted_iota(jnp.int32, (FB * FS, lanes), 0)
    same = (lane % FS) == (freq % FS)
    imag = (lane // FS) % 2 == 1
    zero = freq == 0
    for i in range(HALF):
        row = half * HALF + i
        offset = start_ref[row] - (first_ref[0] + (half - 1) * HALF)
        slot = window - offset
        live = (slot >= 0) & (slot < count_ref[row])
        for k in range(KB):
            pick = (live & (tap == (i * SLOTS + slot) * KB + k)).astype(F32).astype(BF16)
            re = jnp.dot(hat_re, pick, preferred_element_type=F32)
            im = jnp.dot(hat_im, pick, preferred_element_type=F32)
            top = jnp.where(imag, jnp.where(zero, 0.0, -im), re)
            low = jnp.where(imag, jnp.where(zero, im, re), jnp.where(zero, 0.0, im))
            top = jnp.where(same, top, 0.0).astype(BF16).reshape(FB, FS, lanes)
            low = jnp.where(same, low, 0.0).astype(BF16).reshape(FB, FS, lanes)
            at = (i * KB + k) * 2 * FS
            o_ref[0, :, at : at + FS, :] = top
            o_ref[0, :, at + FS : at + 2 * FS, :] = low


def coefs(row_start, row_count, first, kernel, onward, *after):
    smem = pl.BlockSpec(memory_space=pltpu.SMEM)
    taps = HALF * SLOTS * KB
    size = HALF * KB * 2 * FS
    return pl.pallas_call(
        coef_kernel,
        grid=(2,),
        in_specs=[
            smem,
            smem,
            smem,
            pl.BlockSpec((None, taps, NLON), lambda h: (h, 0, 0)),
            pl.BlockSpec((NLON, NLON), lambda h: (0, 0)),
        ]
        + [pl.BlockSpec(memory_space=pl.ANY)] * len(after),
        out_specs=pl.BlockSpec((1, FB, size, WIN * 2 * FS), lambda h: (h, 0, 0, 0)),
        out_shape=jax.ShapeDtypeStruct((2, FB, size, WIN * 2 * FS), BF16),
        compiler_params=params("arbitrary"),
        cost_estimate=cost(8e9, 1e7),
        name="coefs",
    )(row_start, row_count, first, kernel.reshape(2, taps, NLON), onward, *after)


STEP = 4


def mix_kernel(g_ref, a_ref, b_ref, c_ref, theta_ref, back_ref, o_ref, t_ref):
    step = pl.program_id(0)
    theta = [theta_ref[k : k + 1, :] for k in range(KB)]
    for f in range(STEP):
        x = jnp.concatenate([a_ref[f], b_ref[f], c_ref[f]], axis=0)
        p = jnp.dot(g_ref[0, f], x, preferred_element_type=F32)
        for i in range(HALF):
            total = None
            for k in range(KB):
                at = (i * KB + k) * 2 * FS
                term = p[at : at + 2 * FS, :] * theta[k]
                total = term if total is None else total + term
            t_ref[i, pl.ds((step * STEP + f) * 2 * FS, 2 * FS), :] = total.astype(BF16)

    @pl.when(step == FB // STEP - 1)
    def _():
        for pair in range(2):
            y = [
                lax.dot_general(
                    t_ref[pair * 2 + r],
                    back_ref[...],
                    (((0,), (0,)), ((), ())),
                    preferred_element_type=F32,
                ).astype(BF16)
                for r in range(2)
            ]
            for e in range(ENS):
                base = (e * 2 + pair) * 128
                for d in range(LON_DEV):
                    o_ref[d * CH : (d + 1) * CH, base : base + 128] = jnp.concatenate(
                        [v[e * CH : (e + 1) * CH, d * CHUNK : (d + 1) * CHUNK] for v in y], axis=1
                    )


def mix(coef, half, spectra, theta, back):
    size = HALF * KB * 2 * FS
    spec = pl.BlockSpec((STEP, HALF * 2 * FS, COLS), lambda s: (s, 0, 0))
    return pl.pallas_call(
        mix_kernel,
        grid=(FB // STEP,),
        in_specs=[
            pl.BlockSpec((1, STEP, size, WIN * 2 * FS), lambda s: (half, s, 0, 0)),
            spec,
            spec,
            spec,
            pl.BlockSpec((KB, COLS), lambda s: (0, 0)),
            pl.BlockSpec((NLON, NLON), lambda s: (0, 0)),
        ],
        out_specs=pl.BlockSpec((CHAN, PTS), lambda s: (0, 0)),
        out_shape=jax.ShapeDtypeStruct((CHAN, PTS), BF16),
        scratch_shapes=[pltpu.VMEM((HALF, NLON, COLS), BF16)],
        compiler_params=params("arbitrary"),
        cost_estimate=cost(4e9, 1.6e7),
        name="mix",
    )(coef, *spectra, theta, back)


def mlp_kernel(turn_ref, y_ref, x_ref, gain_ref, w_in_ref, b_in_ref, w_out_ref, *rest):
    o_ref = rest[-1]
    at = pl.multiple_of(turn_ref[0] * MID, MID)
    values = jnp.concatenate([y_ref[pl.ds(at, MID), :], y_ref[pl.ds(MID - at, MID), :]], axis=0)
    values = values.astype(F32)
    mean = jnp.mean(values, axis=0, keepdims=True)
    away = values - mean
    var = jnp.mean(away * away, axis=0, keepdims=True)
    normed = (away * lax.rsqrt(var + 1e-5) * gain_ref[...]).astype(BF16)
    hidden = jnp.dot(normed.T, w_in_ref[...], preferred_element_type=F32) + b_in_ref[...]
    hidden = (0.5 * hidden * (1.0 + lax.erf(hidden * np.float32(0.5**0.5)))).astype(BF16)
    branch = jnp.dot(hidden, w_out_ref[...], preferred_element_type=F32)
    x = x_ref[0].reshape(HALF * CHUNK, CHAN).astype(F32)
    o_ref[0] = (x + branch).astype(BF16).reshape(HALF, CHUNK, CHAN)


def mlp(turn, y, fields, half, gain, w_in, b_in, w_out, before=None):
    wide = HALF * CHUNK
    points = pl.BlockSpec((1, HALF, CHUNK, CHAN), lambda e: (e, half, 0, 0))
    whole = lambda *shape: pl.BlockSpec(shape, lambda e: (0, 0))
    extra = () if before is None else (before,)
    return pl.pallas_call(
        mlp_kernel,
        grid=(ENS,),
        in_specs=[
            pl.BlockSpec(memory_space=pltpu.SMEM),
            pl.BlockSpec((CHAN, wide), lambda e: (0, e)),
            points,
            whole(CHAN, 1),
            whole(CHAN, HID),
            whole(1, HID),
            whole(HID, CHAN),
        ]
        + [pl.BlockSpec(memory_space=pl.ANY)] * len(extra),
        out_specs=points,
        out_shape=jax.ShapeDtypeStruct((ENS, ROWS, CHUNK, CHAN), BF16),
        input_output_aliases={7: 0} if extra else {},
        compiler_params=params("arbitrary"),
        cost_estimate=cost(4 * PTS * CHAN * HID, 1.2e7),
        name="mlp",
    )(turn, y, fields, gain, w_in, b_in, w_out, *extra)


def turned(lat):
    return (lat // 2) % 2


def band_perm(lats, lons, step):
    pairs = []
    for lat in range(lats):
        if 0 <= lat + step < lats:
            cross = (turned(lat) ^ turned(lat + step)) * (lons // 2)
            pairs += [(lat * lons + t, (lat + step) * lons + (t ^ cross)) for t in range(lons)]
    return pairs


def shards(fields, kernel, theta, row_start, row_count, norm_gain, w_in, b_in, w_out):
    onward, back = (jnp.asarray(t) for t in tables())
    lats, lons = lax.axis_size("lat"), lax.axis_size("lon")
    lat = lax.axis_index("lat").astype(jnp.int32)
    turn = turned(lat).reshape(1)
    swap = functools.partial(
        lax.all_to_all, axis_name="lon", split_axis=0, concat_axis=0, tiled=True
    )
    shift = lambda v, step: lax.ppermute(v, ("lat", "lon"), band_perm(lats, lons, step))
    other = lax.ppermute(theta, "lon", [(t, t ^ (lons // 2)) for t in range(lons)])
    theta4 = jnp.tile(jnp.where(turn[0] == 1, other, theta), (1, ENS))

    packed_low = pack(turn, fields, 0)
    low = swap(packed_low)
    coef = coefs(row_start, row_count, (lat * ROWS).reshape(1), kernel, onward, packed_low)
    high = swap(pack(turn, fields, 1, coef))
    after = shift(low, -1)
    spec_low = dft(low, onward)
    high, spec_low = lax.optimization_barrier((high, spec_low))
    before = shift(high, 1)
    spec_after = dft(after, onward)
    spec_high = dft(high, onward)
    conv_high = swap(mix(coef, 1, (spec_low, spec_high, spec_after), theta4, back))
    spec_before = dft(before, onward)
    conv_low = swap(mix(coef, 0, (spec_before, spec_low, spec_high), theta4, back))
    rest = (norm_gain[:, None], w_in, b_in[None, :], w_out)
    out = mlp(turn, conv_high, fields, 1, *rest)
    return mlp(turn, conv_low, fields, 0, *rest, before=out)


def solution(mesh):
    placed = (
        P(None, "lat", "lon", None),
        P("lat", None, None, None),
        P(None, "lon"),
        P("lat"),
        P("lat"),
        P(),
        P(),
        P(),
        P(),
    )
    return jax.shard_map(
        shards, mesh=mesh, in_specs=placed, out_specs=P(None, "lat", "lon", None), check_vma=False
    )
```

```python
import functools

import jax
import jax.numpy as jnp
import ml_dtypes
import numpy as np
from jax import lax
from jax.experimental import pallas as pl
from jax.experimental.pallas import tpu as pltpu
from jax.sharding import PartitionSpec as P

BF16 = jnp.bfloat16
F32 = jnp.float32

LON_DEV = 8
ROWS = 8
HALF = 4
ENS = 4
CHUNK = 64
CHAN = 640
CH = 80
COLS = ENS * CH
NLON = 512
SLOTS = 9
KB = 3
FB = 16
FS = 16
WIN = 12
PTS = ENS * HALF * CHUNK
HID = 1280
MID = CHAN // 2
LIMIT = 58 * 1024 * 1024
GROUP = 2
ANY = pl.BlockSpec(memory_space=pl.ANY)
SMEM = pl.BlockSpec(memory_space=pltpu.SMEM)
VMEM = pl.BlockSpec(memory_space=pltpu.VMEM)


def tables():
    point = np.arange(NLON)
    freq = np.arange(NLON // 2)
    angle = 2.0 * np.pi * ((freq[:, None] * point[None, :]) % NLON) / NLON
    re, im = np.cos(angle), -np.sin(angle)
    im[0] = np.cos(np.pi * point)
    weight = np.full((NLON // 2, 1), 2.0 / NLON)
    weight[0] = 1.0 / NLON
    onward = np.stack([re.reshape(FB, FS, NLON), im.reshape(FB, FS, NLON)], axis=1)
    back = np.stack(
        [(re * weight).reshape(FB, FS, NLON), (im * weight).reshape(FB, FS, NLON)], axis=1
    )
    return (
        onward.reshape(NLON, NLON).astype(ml_dtypes.bfloat16),
        back.reshape(NLON, NLON).astype(ml_dtypes.bfloat16),
    )


def params(*semantics):
    return pltpu.CompilerParams(vmem_limit_bytes=LIMIT, dimension_semantics=semantics)


def near(value):
    return pltpu.with_memory_space_constraint(value, pltpu.VMEM)


def far(value):
    return pltpu.with_memory_space_constraint(value, pltpu.HBM)


def cost(flops, nbytes):
    return pl.CostEstimate(flops=int(flops), bytes_accessed=int(nbytes), transcendentals=0)


def pack_kernel(half, turn_ref, x_ref, *rest):
    o_ref, x_buf, o_buf, x_sem, o_sem = rest[-5:]
    wide = HALF * CHUNK
    copies = [
        pltpu.make_async_copy(x_ref.at[e, pl.ds(half * HALF, HALF)], x_buf.at[e], x_sem.at[e])
        for e in range(ENS)
    ]
    for c in copies:
        c.start()
    at = pl.multiple_of(turn_ref[0] * MID, MID)
    outs = []
    for e in range(ENS):
        copies[e].wait()
        x = x_buf[e].reshape(wide, CHAN).T
        lanes = slice(e * wide, (e + 1) * wide)
        o_buf[pl.ds(at, MID), lanes] = x[:MID]
        o_buf[pl.ds(MID - at, MID), lanes] = x[MID:]
        outs.append(pltpu.make_async_copy(o_buf.at[:, lanes], o_ref.at[:, lanes], o_sem.at[e]))
        outs[e].start()
    for c in outs:
        c.wait()


def pack(turn, fields, half, *after):
    return pl.pallas_call(
        functools.partial(pack_kernel, half),
        in_specs=[pl.BlockSpec(memory_space=pltpu.SMEM)] + [ANY] * (1 + len(after)),
        out_specs=ANY,
        out_shape=jax.ShapeDtypeStruct((CHAN, PTS), BF16),
        scratch_shapes=[
            pltpu.VMEM((ENS, HALF, CHUNK, CHAN), BF16),
            pltpu.VMEM((CHAN, PTS), BF16),
            pltpu.SemaphoreType.DMA((ENS,)),
            pltpu.SemaphoreType.DMA((ENS,)),
        ],
        compiler_params=params(),
        cost_estimate=cost(0, 4 * CHAN * PTS),
        name="pack",
    )(turn, fields, *after)


def dft_rows(x_ref, w, o_ref, at):
    for pair in range(2):
        rows = [[], []]
        for e in range(ENS):
            parts = [[], []]
            base = (e * 2 + pair) * 128
            for d in range(LON_DEV):
                tile = x_ref[d * CH : (d + 1) * CH, base : base + 128]
                parts[0].append(tile[:, :CHUNK])
                parts[1].append(tile[:, CHUNK:])
            for r in range(2):
                rows[r].append(jnp.concatenate(parts[r], axis=1))
        for r in range(2):
            x = jnp.concatenate(rows[r], axis=0)
            s = lax.dot_general(w, x, (((1,), (1,)), ((), ())), preferred_element_type=F32)
            row = at + (pair * 2 + r) * 2 * FS
            o_ref[:, row : row + 2 * FS, :] = s.astype(BF16).reshape(FB, 2 * FS, COLS)


def dft_kernel(x_ref, w_ref, o_ref):
    dft_rows(x_ref, w_ref[...], o_ref, 0)


def dft(received, onward):
    return pl.pallas_call(
        dft_kernel,
        out_shape=jax.ShapeDtypeStruct((FB, HALF * 2 * FS, COLS), BF16),
        compiler_params=params(),
        cost_estimate=cost(2 * HALF * NLON * NLON * COLS, 8 * CHAN * PTS),
        name="dft",
    )(far(received), onward)


def coef_kernel(start_ref, count_ref, first_ref, k_ref, w_ref, *rest):
    o_ref = rest[-1]
    half = pl.program_id(0)
    kern = k_ref[...].astype(BF16)
    hat = lax.dot_general(w_ref[...], kern, (((1,), (1,)), ((), ())), preferred_element_type=F32)
    hat = hat.astype(BF16).reshape(FB, 2, FS, SLOTS * KB * HALF)
    hat_re = hat[:, 0].reshape(FB * FS, SLOTS * KB * HALF)
    hat_im = hat[:, 1].reshape(FB * FS, SLOTS * KB * HALF)
    lanes = WIN * 2 * FS
    taps = SLOTS * KB * HALF
    tap = lax.broadcasted_iota(jnp.int32, (taps, lanes), 0)
    window = lax.broadcasted_iota(jnp.int32, (taps, lanes), 1) // (2 * FS)
    lane = lax.broadcasted_iota(jnp.int32, (FB * FS, lanes), 1)
    freq = lax.broadcasted_iota(jnp.int32, (FB * FS, lanes), 0)
    same = (lane % FS) == (freq % FS)
    imag = (lane // FS) % 2 == 1
    zero = freq == 0
    for i in range(HALF):
        row = half * HALF + i
        offset = start_ref[row] - (first_ref[0] + (half - 1) * HALF)
        slot = window - offset
        live = (slot >= 0) & (slot < count_ref[row])
        for k in range(KB):
            pick = (live & (tap == (i * SLOTS + slot) * KB + k)).astype(F32).astype(BF16)
            re = jnp.dot(hat_re, pick, preferred_element_type=F32)
            im = jnp.dot(hat_im, pick, preferred_element_type=F32)
            top = jnp.where(imag, jnp.where(zero, 0.0, -im), re)
            low = jnp.where(imag, jnp.where(zero, im, re), jnp.where(zero, 0.0, im))
            top = jnp.where(same, top, 0.0).astype(BF16).reshape(FB, FS, lanes)
            low = jnp.where(same, low, 0.0).astype(BF16).reshape(FB, FS, lanes)
            at = (i * KB + k) * 2 * FS
            o_ref[0, :, at : at + FS, :] = top
            o_ref[0, :, at + FS : at + 2 * FS, :] = low


def coefs(row_start, row_count, first, kernel, onward, *after):
    smem = pl.BlockSpec(memory_space=pltpu.SMEM)
    taps = HALF * SLOTS * KB
    size = HALF * KB * 2 * FS
    return pl.pallas_call(
        coef_kernel,
        grid=(2,),
        in_specs=[
            smem,
            smem,
            smem,
            pl.BlockSpec((None, taps, NLON), lambda h: (h, 0, 0)),
            pl.BlockSpec((NLON, NLON), lambda h: (0, 0)),
        ]
        + [pl.BlockSpec(memory_space=pl.ANY)] * len(after),
        out_specs=pl.BlockSpec((1, FB, size, WIN * 2 * FS), lambda h: (h, 0, 0, 0)),
        out_shape=jax.ShapeDtypeStruct((2, FB, size, WIN * 2 * FS), BF16),
        compiler_params=params("arbitrary"),
        cost_estimate=cost(8e9, 1e7),
        name="coefs",
    )(row_start, row_count, first, kernel.reshape(2, taps, NLON), onward, *after)


STEP = 4
STEPS = FB // STEP


def conv_kernel(
    half, g_ref, low_ref, high_ref, halo_ref, theta_ref, w_ref, back_ref, o_ref, *rest
):
    g_buf, s_buf, w_buf, t_buf, g_sem, low_sem, w_sem = rest
    band = HALF * 2 * FS
    halo_at, low_at, high_at = (2 * band, 0, band) if half else (0, band, 2 * band)
    ws = [
        pltpu.make_async_copy(ref, w_buf.at[n], w_sem.at[n]) for n, ref in enumerate((w_ref, back_ref))
    ]
    ws[0].start()
    gs, lows = [], []
    for s in range(STEPS):
        part = pl.ds(s * STEP, STEP)
        gs.append(pltpu.make_async_copy(g_ref.at[half, part], g_buf.at[part], g_sem.at[s]))
        lows.append(
            pltpu.make_async_copy(
                low_ref.at[part], s_buf.at[part, pl.ds(low_at, band)], low_sem.at[s]
            )
        )
        gs[s].start()
        lows[s].start()
    ws[1].start()
    ws[0].wait()
    dft_rows(high_ref, w_buf[0], s_buf, high_at)
    dft_rows(halo_ref, w_buf[0], s_buf, halo_at)
    theta = [theta_ref[k : k + 1, :] for k in range(KB)]
    for step in range(STEPS):
        gs[step].wait()
        lows[step].wait()
        for block in range(step * STEP, (step + 1) * STEP):
            p = jnp.dot(g_buf[block], s_buf[block], preferred_element_type=F32)
            for i in range(HALF):
                total = None
                for k in range(KB):
                    at = (i * KB + k) * 2 * FS
                    term = p[at : at + 2 * FS, :] * theta[k]
                    total = term if total is None else total + term
                t_buf[i, block * 2 * FS : (block + 1) * 2 * FS, :] = total.astype(BF16)
    ws[1].wait()
    for pair in range(2):
        y = [
            lax.dot_general(
                t_buf[pair * 2 + r],
                w_buf[1],
                (((0,), (0,)), ((), ())),
                preferred_element_type=F32,
            ).astype(BF16)
            for r in range(2)
        ]
        for e in range(ENS):
            base = (e * 2 + pair) * 128
            for d in range(LON_DEV):
                o_ref[d * CH : (d + 1) * CH, base : base + 128] = jnp.concatenate(
                    [v[e * CH : (e + 1) * CH, d * CHUNK : (d + 1) * CHUNK] for v in y], axis=1
                )


def conv(coef, half, spec_low, high, halo, theta, onward, back):
    size = HALF * KB * 2 * FS
    span = WIN * 2 * FS
    return pl.pallas_call(
        functools.partial(conv_kernel, half),
        in_specs=[ANY, ANY, VMEM, VMEM, VMEM, ANY, ANY],
        out_specs=VMEM,
        out_shape=pltpu.VMEM((CHAN, PTS), BF16),
        scratch_shapes=[
            pltpu.VMEM((FB, size, span), BF16),
            pltpu.VMEM((FB, span, COLS), BF16),
            pltpu.VMEM((2, NLON, NLON), BF16),
            pltpu.VMEM((HALF, NLON, COLS), BF16),
            pltpu.SemaphoreType.DMA((STEPS,)),
            pltpu.SemaphoreType.DMA((STEPS,)),
            pltpu.SemaphoreType.DMA((2,)),
        ],
        compiler_params=params(),
        cost_estimate=cost(6e9, 1.2e7),
        name="conv",
    )(coef, spec_low, near(high), near(halo), theta, onward, back)


def mlp_kernel(half, turn_ref, y_ref, x_ref, gain_ref, w_in_ref, b_in_ref, w_out_ref, *rest):
    o_ref, x_buf, w_in_buf, w_out_buf, o_buf, x_sem, w_sem, o_sem = rest[-8:]
    wide = HALF * CHUNK
    rows = pl.ds(half * HALF, HALF)
    first = pltpu.make_async_copy(w_in_ref, w_in_buf, w_sem.at[0])
    second = pltpu.make_async_copy(w_out_ref, w_out_buf, w_sem.at[1])
    xs = [
        pltpu.make_async_copy(x_ref.at[e, rows], x_buf.at[e], x_sem.at[e]) for e in range(ENS)
    ]
    for c in [first, second, *xs]:
        c.start()
    at = pl.multiple_of(turn_ref[0] * MID, MID)
    outs = []
    for part in range(ENS // GROUP):
        lanes = slice(part * GROUP * wide, (part + 1) * GROUP * wide)
        values = jnp.concatenate(
            [y_ref[pl.ds(at, MID), lanes], y_ref[pl.ds(MID - at, MID), lanes]], axis=0
        ).astype(F32)
        mean = jnp.mean(values, axis=0, keepdims=True)
        away = values - mean
        var = jnp.mean(away * away, axis=0, keepdims=True)
        normed = (away * lax.rsqrt(var + 1e-5) * gain_ref[...]).astype(BF16).T
        if part == 0:
            first.wait()
        hidden = jnp.dot(normed, w_in_buf[...], preferred_element_type=F32) + b_in_ref[...]
        hidden = (0.5 * hidden * (1.0 + lax.erf(hidden * np.float32(0.5**0.5)))).astype(BF16)
        if part == 0:
            second.wait()
        branch = jnp.dot(hidden, w_out_buf[...], preferred_element_type=F32)
        for g in range(GROUP):
            e = part * GROUP + g
            xs[e].wait()
            x = x_buf[e].reshape(wide, CHAN).astype(F32)
            o_buf[e] = (
                (x + branch[g * wide : (g + 1) * wide]).astype(BF16).reshape(HALF, CHUNK, CHAN)
            )
            outs.append(pltpu.make_async_copy(o_buf.at[e], o_ref.at[e, rows], o_sem.at[e]))
            outs[e].start()
    for c in outs:
        c.wait()


def mlp(turn, y, fields, half, gain, w_in, b_in, w_out, before=None):
    extra = () if before is None else (before,)
    points = (ENS, HALF, CHUNK, CHAN)
    sems = pltpu.SemaphoreType.DMA
    return pl.pallas_call(
        functools.partial(mlp_kernel, half),
        in_specs=[SMEM, VMEM, ANY, VMEM, ANY, VMEM, ANY] + [ANY] * len(extra),
        out_specs=ANY,
        out_shape=jax.ShapeDtypeStruct((ENS, ROWS, CHUNK, CHAN), BF16),
        input_output_aliases={7: 0} if extra else {},
        scratch_shapes=[
            pltpu.VMEM(points, BF16),
            pltpu.VMEM((CHAN, HID), BF16),
            pltpu.VMEM((HID, CHAN), BF16),
            pltpu.VMEM(points, BF16),
            sems((ENS,)),
            sems((2,)),
            sems((ENS,)),
        ],
        compiler_params=params(),
        cost_estimate=cost(4 * PTS * CHAN * HID, 1.2e7),
        name="mlp",
    )(turn, near(y), fields, gain, w_in, b_in, w_out, *extra)


def turned(lat):
    return (lat // 2) % 2


def band_perm(lats, lons, step):
    pairs = []
    for lat in range(lats):
        if 0 <= lat + step < lats:
            cross = (turned(lat) ^ turned(lat + step)) * (lons // 2)
            pairs += [(lat * lons + t, (lat + step) * lons + (t ^ cross)) for t in range(lons)]
    return pairs


def shards(fields, kernel, theta, row_start, row_count, norm_gain, w_in, b_in, w_out):
    onward, back = (jnp.asarray(t) for t in tables())
    lats, lons = lax.axis_size("lat"), lax.axis_size("lon")
    lat = lax.axis_index("lat").astype(jnp.int32)
    turn = turned(lat).reshape(1)
    swap = functools.partial(
        lax.all_to_all, axis_name="lon", split_axis=0, concat_axis=0, tiled=True
    )
    shift = lambda v, step: lax.ppermute(v, ("lat", "lon"), band_perm(lats, lons, step))
    other = lax.ppermute(theta, "lon", [(t, t ^ (lons // 2)) for t in range(lons)])
    theta4 = jnp.tile(jnp.where(turn[0] == 1, other, theta), (1, ENS))

    packed_low = pack(turn, fields, 0)
    low = swap(packed_low)
    coef = coefs(row_start, row_count, (lat * ROWS).reshape(1), kernel, onward, packed_low)
    high = swap(pack(turn, fields, 1, coef))
    after = shift(low, -1)
    spec_low = dft(low, onward)
    high, spec_low = lax.optimization_barrier((high, spec_low))
    before = shift(high, 1)
    conv_high = swap(conv(coef, 1, spec_low, high, after, theta4, onward, back))
    conv_low = swap(conv(coef, 0, spec_low, high, before, theta4, onward, back))
    rest = (norm_gain[:, None], w_in, b_in[None, :], w_out)
    out = mlp(turn, conv_high, fields, 1, *rest)
    return mlp(turn, conv_low, fields, 0, *rest, before=out)


def solution(mesh):
    placed = (
        P(None, "lat", "lon", None),
        P("lat", None, None, None),
        P(None, "lon"),
        P("lat"),
        P("lat"),
        P(),
        P(),
        P(),
        P(),
    )
    return jax.shard_map(
        shards, mesh=mesh, in_specs=placed, out_specs=P(None, "lat", "lon", None), check_vma=False
    )
```

```python
import functools

import jax
import jax.numpy as jnp
import ml_dtypes
import numpy as np
from jax import lax
from jax.experimental import pallas as pl
from jax.experimental.pallas import tpu as pltpu
from jax.sharding import PartitionSpec as P

BF16 = jnp.bfloat16
F32 = jnp.float32

LON_DEV = 8
ROWS = 8
HALF = 4
ENS = 4
CHUNK = 64
CHAN = 640
CH = 80
COLS = ENS * CH
NLON = 512
SLOTS = 9
KB = 3
FB = 16
FS = 16
BAND = HALF * 2 * FS
WIN = 12
PTS = ENS * HALF * CHUNK
HID = 1280
MID = CHAN // 2
LIMIT = 58 * 1024 * 1024
GROUP = 2
ANY = pl.BlockSpec(memory_space=pl.ANY)
SMEM = pl.BlockSpec(memory_space=pltpu.SMEM)
VMEM = pl.BlockSpec(memory_space=pltpu.VMEM)


def tables():
    point = np.arange(NLON)
    freq = np.arange(NLON // 2)
    angle = 2.0 * np.pi * ((freq[:, None] * point[None, :]) % NLON) / NLON
    re, im = np.cos(angle), -np.sin(angle)
    im[0] = np.cos(np.pi * point)
    weight = np.full((NLON // 2, 1), 2.0 / NLON)
    weight[0] = 1.0 / NLON
    onward = np.stack([re.reshape(FB, FS, NLON), im.reshape(FB, FS, NLON)], axis=1)
    back = np.stack(
        [(re * weight).reshape(FB, FS, NLON), (im * weight).reshape(FB, FS, NLON)], axis=1
    )
    return (
        onward.reshape(NLON, NLON).astype(ml_dtypes.bfloat16),
        back.reshape(NLON, NLON).astype(ml_dtypes.bfloat16),
    )


def params(*semantics):
    return pltpu.CompilerParams(vmem_limit_bytes=LIMIT, dimension_semantics=semantics)


def near(value):
    return pltpu.with_memory_space_constraint(value, pltpu.VMEM)


def block_of(index):
    return pl.ds(pl.multiple_of(index * CH, CH), CH)


def cost(flops, nbytes):
    return pl.CostEstimate(flops=int(flops), bytes_accessed=int(nbytes), transcendentals=0)


def pack_kernel(half, turn_ref, x_ref, *rest):
    o_ref, x_buf, o_buf, x_sem, o_sem = rest[-5:]
    wide = HALF * CHUNK
    copies = [
        pltpu.make_async_copy(x_ref.at[e, pl.ds(half * HALF, HALF)], x_buf.at[e], x_sem.at[e])
        for e in range(ENS)
    ]
    for c in copies:
        c.start()
    at = pl.multiple_of(turn_ref[0] * MID, MID)
    outs = []
    for e in range(ENS):
        copies[e].wait()
        x = x_buf[e].reshape(wide, CHAN).T
        lanes = slice(e * wide, (e + 1) * wide)
        o_buf[pl.ds(at, MID), lanes] = x[:MID]
        o_buf[pl.ds(MID - at, MID), lanes] = x[MID:]
        outs.append(pltpu.make_async_copy(o_buf.at[:, lanes], o_ref.at[:, lanes], o_sem.at[e]))
        outs[e].start()
    for c in outs:
        c.wait()


def pack(turn, fields, half, *after):
    return pl.pallas_call(
        functools.partial(pack_kernel, half),
        in_specs=[pl.BlockSpec(memory_space=pltpu.SMEM)] + [ANY] * (1 + len(after)),
        out_specs=ANY,
        out_shape=jax.ShapeDtypeStruct((CHAN, PTS), BF16),
        scratch_shapes=[
            pltpu.VMEM((ENS, HALF, CHUNK, CHAN), BF16),
            pltpu.VMEM((CHAN, PTS), BF16),
            pltpu.SemaphoreType.DMA((ENS,)),
            pltpu.SemaphoreType.DMA((ENS,)),
        ],
        compiler_params=params(),
        cost_estimate=cost(0, 4 * CHAN * PTS),
        name="pack",
    )(turn, fields, *after)


def dft_rows(x_ref, w, o_ref, at):
    for pair in range(2):
        rows = [[], []]
        for e in range(ENS):
            parts = [[], []]
            base = (e * 2 + pair) * 128
            for d in range(LON_DEV):
                tile = x_ref[d * CH : (d + 1) * CH, base : base + 128]
                parts[0].append(tile[:, :CHUNK])
                parts[1].append(tile[:, CHUNK:])
            for r in range(2):
                rows[r].append(jnp.concatenate(parts[r], axis=1))
        for r in range(2):
            x = jnp.concatenate(rows[r], axis=0)
            s = lax.dot_general(w, x, (((1,), (1,)), ((), ())), preferred_element_type=F32)
            row = at + (pair * 2 + r) * 2 * FS
            o_ref[:, row : row + 2 * FS, :] = s.astype(BF16).reshape(FB, 2 * FS, COLS)


def coef_kernel(start_ref, count_ref, first_ref, k_ref, w_ref, *rest):
    low_ref, rest_ref = rest[-2:]
    half = pl.program_id(0)
    kern = k_ref[...].astype(BF16)
    hat = lax.dot_general(w_ref[...], kern, (((1,), (1,)), ((), ())), preferred_element_type=F32)
    hat = hat.astype(BF16).reshape(FB, 2, FS, SLOTS * KB * HALF)
    hat_re = hat[:, 0].reshape(FB * FS, SLOTS * KB * HALF)
    hat_im = hat[:, 1].reshape(FB * FS, SLOTS * KB * HALF)
    lanes = WIN * 2 * FS
    taps = SLOTS * KB * HALF
    tap = lax.broadcasted_iota(jnp.int32, (taps, lanes), 0)
    window = lax.broadcasted_iota(jnp.int32, (taps, lanes), 1) // (2 * FS)
    window = jnp.where((half == 0) & (window < 2 * HALF), window ^ HALF, window)
    lane = lax.broadcasted_iota(jnp.int32, (FB * FS, lanes), 1)
    freq = lax.broadcasted_iota(jnp.int32, (FB * FS, lanes), 0)
    same = (lane % FS) == (freq % FS)
    imag = (lane // FS) % 2 == 1
    zero = freq == 0
    for i in range(HALF):
        row = half * HALF + i
        offset = start_ref[row] - (first_ref[0] + (half - 1) * HALF)
        slot = window - offset
        live = (slot >= 0) & (slot < count_ref[row])
        for k in range(KB):
            pick = (live & (tap == (i * SLOTS + slot) * KB + k)).astype(F32).astype(BF16)
            re = jnp.dot(hat_re, pick, preferred_element_type=F32)
            im = jnp.dot(hat_im, pick, preferred_element_type=F32)
            top = jnp.where(imag, jnp.where(zero, 0.0, -im), re)
            low = jnp.where(imag, jnp.where(zero, im, re), jnp.where(zero, 0.0, im))
            top = jnp.where(same, top, 0.0).astype(BF16).reshape(FB, FS, lanes)
            low = jnp.where(same, low, 0.0).astype(BF16).reshape(FB, FS, lanes)
            at = (i * KB + k) * 2 * FS
            low_ref[0, :, at : at + FS, :] = top[:, :, :BAND]
            rest_ref[0, :, at : at + FS, :] = top[:, :, BAND:]
            low_ref[0, :, at + FS : at + 2 * FS, :] = low[:, :, :BAND]
            rest_ref[0, :, at + FS : at + 2 * FS, :] = low[:, :, BAND:]


def coefs(row_start, row_count, first, kernel, onward, *after):
    smem = pl.BlockSpec(memory_space=pltpu.SMEM)
    taps = HALF * SLOTS * KB
    size = HALF * KB * 2 * FS
    return pl.pallas_call(
        coef_kernel,
        grid=(2,),
        in_specs=[
            smem,
            smem,
            smem,
            pl.BlockSpec((None, taps, NLON), lambda h: (h, 0, 0)),
            pl.BlockSpec((NLON, NLON), lambda h: (0, 0)),
        ]
        + [pl.BlockSpec(memory_space=pl.ANY)] * len(after),
        out_specs=[pl.BlockSpec((1, FB, size, n), lambda h: (h, 0, 0, 0)) for n in (BAND, 2 * BAND)],
        out_shape=[jax.ShapeDtypeStruct((2, FB, size, n), BF16) for n in (BAND, 2 * BAND)],
        compiler_params=params("arbitrary"),
        cost_estimate=cost(8e9, 1e7),
        name="coefs",
    )(row_start, row_count, first, kernel.reshape(2, taps, NLON), onward, *after)


def combine(p, theta):
    rows = []
    for i in range(HALF):
        total = None
        for k in range(KB):
            at = (i * KB + k) * 2 * FS
            term = p[at : at + 2 * FS, :] * theta[k]
            total = term if total is None else total + term
        rows.append(total)
    return rows


def low_kernel(x_ref, w_ref, g_ref, theta_ref, o_ref, s_buf):
    @pl.when(pl.program_id(0) == 0)
    def _():
        dft_rows(x_ref, w_ref[...], s_buf, 0)

    theta = [theta_ref[k : k + 1, :] for k in range(KB)]
    for block in range(FB):
        p = jnp.dot(g_ref[0, block], s_buf[block], preferred_element_type=F32)
        for i, row in enumerate(combine(p, theta)):
            o_ref[0, i, block * 2 * FS : (block + 1) * 2 * FS, :] = row


def low_share(received, onward, coef_low, theta):
    whole = lambda *shape: pl.BlockSpec(shape, lambda h: (0,) * len(shape))
    return pl.pallas_call(
        low_kernel,
        grid=(2,),
        in_specs=[
            whole(CHAN, PTS),
            whole(NLON, NLON),
            pl.BlockSpec((1, FB, HALF * KB * 2 * FS, BAND), lambda h: (h, 0, 0, 0)),
            whole(KB, COLS),
        ],
        out_specs=pl.BlockSpec((1, HALF, NLON, COLS), lambda h: (h, 0, 0, 0)),
        out_shape=jax.ShapeDtypeStruct((2, HALF, NLON, COLS), F32),
        scratch_shapes=[pltpu.VMEM((FB, BAND, COLS), BF16)],
        compiler_params=params("arbitrary"),
        cost_estimate=cost(2e9, 8e6),
        name="low",
    )(received, onward, coef_low, theta)


STEP = 4
STEPS = FB // STEP


def conv_kernel(
    half, me_ref, g_ref, low_ref, high_ref, halo_ref, theta_ref, w_ref, back_ref, *rest
):
    count = len(rest) - 11
    pieces, rest = rest[:count], rest[count:]
    o_buf, g_buf, s_buf, l_buf, x_buf, w_buf, t_buf, g_sem, l_sem, w_sem, o_sem = rest
    halo_at, high_at = (BAND, 0) if half else (0, BAND)
    moves = [(w_ref, w_buf.at[0]), (halo_ref, x_buf.at[1]), (back_ref, w_buf.at[1])]
    moves += [] if half else [(high_ref, x_buf.at[0])]
    ws = [pltpu.make_async_copy(ref, to, w_sem.at[n]) for n, (ref, to) in enumerate(moves)]
    gs, lows = [], []
    for s in range(STEPS):
        part = pl.ds(s * STEP, STEP)
        rows = pl.ds(s * STEP * 2 * FS, STEP * 2 * FS)
        gs.append(pltpu.make_async_copy(g_ref.at[half, part], g_buf.at[part], g_sem.at[s]))
        lows.append(pltpu.make_async_copy(low_ref.at[half, :, rows], l_buf.at[:, rows], l_sem.at[s]))
    for c in ws[:1] + ws[3:] + ws[1:2]:
        c.start()
    for s in range(STEPS):
        gs[s].start()
        lows[s].start()
    ws[2].start()
    for c in ws[:1] + ws[3:]:
        c.wait()
    dft_rows(high_ref if half else x_buf.at[0], w_buf[0], s_buf, high_at)
    ws[1].wait()
    dft_rows(x_buf.at[1], w_buf[0], s_buf, halo_at)
    theta = [theta_ref[k : k + 1, :] for k in range(KB)]
    for step in range(STEPS):
        gs[step].wait()
        lows[step].wait()
        for block in range(step * STEP, (step + 1) * STEP):
            p = jnp.dot(g_buf[block], s_buf[block], preferred_element_type=F32)
            rows = slice(block * 2 * FS, (block + 1) * 2 * FS)
            for i, row in enumerate(combine(p, theta)):
                t_buf[i, rows, :] = (row + l_buf[i, rows, :]).astype(BF16)
    ws[2].wait()
    outs = []
    for pair in range(2):
        y = [
            lax.dot_general(
                t_buf[pair * 2 + r],
                w_buf[1],
                (((0,), (0,)), ((), ())),
                preferred_element_type=F32,
            ).astype(BF16)
            for r in range(2)
        ]
        for e in range(ENS):
            base = (e * 2 + pair) * 128
            for d in range(LON_DEV):
                o_buf[d * CH : (d + 1) * CH, base : base + 128] = jnp.concatenate(
                    [v[e * CH : (e + 1) * CH, d * CHUNK : (d + 1) * CHUNK] for v in y], axis=1
                )
            if count == 1:
                lanes = slice(base, base + 128)
                outs.append(
                    pltpu.make_async_copy(
                        o_buf.at[:, lanes], pieces[0].at[:, lanes], o_sem.at[pair * ENS + e]
                    )
                )
                outs[-1].start()
    if count > 1:
        outs = [
            pltpu.make_async_copy(o_buf.at[block_of(me_ref[0] ^ k)], piece, o_sem.at[k])
            for k, piece in enumerate(pieces)
        ]
        for c in outs:
            c.start()
    for c in outs:
        c.wait()


def conv(me, coef, half, low, high, halo, theta, onward, back, split):
    size = HALF * KB * 2 * FS
    sems = pltpu.SemaphoreType.DMA
    shape = (CH, PTS) if split else (CHAN, PTS)
    count = LON_DEV if split else 1
    return pl.pallas_call(
        functools.partial(conv_kernel, half),
        in_specs=[SMEM, ANY, ANY, VMEM if half else ANY, ANY, VMEM, ANY, ANY],
        out_specs=[ANY] * count,
        out_shape=[jax.ShapeDtypeStruct(shape, BF16)] * count,
        scratch_shapes=[
            pltpu.VMEM((CHAN, PTS), BF16),
            pltpu.VMEM((FB, size, 2 * BAND), BF16),
            pltpu.VMEM((FB, 2 * BAND, COLS), BF16),
            pltpu.VMEM((HALF, NLON, COLS), F32),
            pltpu.VMEM((2, CHAN, PTS), BF16),
            pltpu.VMEM((2, NLON, NLON), BF16),
            pltpu.VMEM((HALF, NLON, COLS), BF16),
            sems((STEPS,)),
            sems((STEPS,)),
            sems((4,)),
            sems((LON_DEV,)),
        ],
        compiler_params=params(),
        cost_estimate=cost(6e9, 1.2e7),
        name="conv",
    )(me, coef, low, near(high) if half else high, halo, theta, onward, back)


def mlp_kernel(half, count, me_ref, turn_ref, *refs):
    pieces, refs = refs[:count], refs[count:]
    x_ref, gain_ref, w_in_ref, b_in_ref, w_out_ref, *rest = refs
    o_ref, y_buf, x_buf, w_in_buf, w_out_buf, o_buf, y_sem, x_sem, w_sem, o_sem = rest[-10:]
    turned_by = turn_ref[0] * (LON_DEV // 2)
    ys = [
        pltpu.make_async_copy(piece, y_buf.at[block_of(me_ref[0] ^ k ^ turned_by)], y_sem.at[k])
        for k, piece in enumerate(pieces)
        if count > 1
    ]
    wide = HALF * CHUNK
    rows = pl.ds(half * HALF, HALF)
    first = pltpu.make_async_copy(w_in_ref, w_in_buf, w_sem.at[0])
    second = pltpu.make_async_copy(w_out_ref, w_out_buf, w_sem.at[1])
    xs = [
        pltpu.make_async_copy(x_ref.at[e, rows], x_buf.at[e], x_sem.at[e]) for e in range(ENS)
    ]
    for c in [*ys, first, second, *xs]:
        c.start()
    for c in ys:
        c.wait()
    at = pl.multiple_of(turn_ref[0] * MID, MID)
    outs = []
    for part in range(ENS // GROUP):
        lanes = slice(part * GROUP * wide, (part + 1) * GROUP * wide)
        if count > 1:
            values = y_buf[:, lanes].astype(F32)
        else:
            y_ref = pieces[0]
            values = jnp.concatenate(
                [y_ref[pl.ds(at, MID), lanes], y_ref[pl.ds(MID - at, MID), lanes]], axis=0
            ).astype(F32)
        mean = jnp.mean(values, axis=0, keepdims=True)
        away = values - mean
        var = jnp.mean(away * away, axis=0, keepdims=True)
        normed = (away * lax.rsqrt(var + 1e-5) * gain_ref[...]).astype(BF16).T
        if part == 0:
            first.wait()
        hidden = jnp.dot(normed, w_in_buf[...], preferred_element_type=F32) + b_in_ref[...]
        hidden = (0.5 * hidden * (1.0 + lax.erf(hidden * np.float32(0.5**0.5)))).astype(BF16)
        if part == 0:
            second.wait()
        branch = jnp.dot(hidden, w_out_buf[...], preferred_element_type=F32)
        for g in range(GROUP):
            e = part * GROUP + g
            xs[e].wait()
            x = x_buf[e].reshape(wide, CHAN).astype(F32)
            o_buf[e] = (
                (x + branch[g * wide : (g + 1) * wide]).astype(BF16).reshape(HALF, CHUNK, CHAN)
            )
            outs.append(pltpu.make_async_copy(o_buf.at[e], o_ref.at[e, rows], o_sem.at[e]))
            outs[e].start()
    for c in outs:
        c.wait()


def mlp(me, turn, ys, fields, half, gain, w_in, b_in, w_out, before=None):
    extra = () if before is None else (before,)
    count = len(ys)
    points = (ENS, HALF, CHUNK, CHAN)
    sems = pltpu.SemaphoreType.DMA
    return pl.pallas_call(
        functools.partial(mlp_kernel, half, count),
        in_specs=[SMEM, SMEM]
        + ([ANY] * count if count > 1 else [VMEM])
        + [ANY, VMEM, ANY, VMEM, ANY]
        + [ANY] * len(extra),
        out_specs=ANY,
        out_shape=jax.ShapeDtypeStruct((ENS, ROWS, CHUNK, CHAN), BF16),
        input_output_aliases={count + 7: 0} if extra else {},
        scratch_shapes=[
            pltpu.VMEM((CHAN, PTS) if count > 1 else (16, 128), BF16),
            pltpu.VMEM(points, BF16),
            pltpu.VMEM((CHAN, HID), BF16),
            pltpu.VMEM((HID, CHAN), BF16),
            pltpu.VMEM(points, BF16),
            sems((LON_DEV,)),
            sems((ENS,)),
            sems((2,)),
            sems((ENS,)),
        ],
        compiler_params=params(),
        cost_estimate=cost(4 * PTS * CHAN * HID, 1.2e7),
        name="mlp",
    )(me, turn, *(ys if count > 1 else [near(ys[0])]), fields, gain, w_in, b_in, w_out, *extra)


def turned(lat):
    return (lat // 2) % 2


def band_perm(lats, lons, step):
    pairs = []
    for lat in range(lats):
        if 0 <= lat + step < lats:
            cross = (turned(lat) ^ turned(lat + step)) * (lons // 2)
            pairs += [(lat * lons + t, (lat + step) * lons + (t ^ cross)) for t in range(lons)]
    return pairs


def shards(fields, kernel, theta, row_start, row_count, norm_gain, w_in, b_in, w_out):
    onward, back = (jnp.asarray(t) for t in tables())
    lats, lons = lax.axis_size("lat"), lax.axis_size("lon")
    lat = lax.axis_index("lat").astype(jnp.int32)
    turn = turned(lat).reshape(1)
    me = lax.axis_index("lon").astype(jnp.int32).reshape(1)
    swap = functools.partial(
        lax.all_to_all, axis_name="lon", split_axis=0, concat_axis=0, tiled=True
    )
    shift = lambda v, step: lax.ppermute(v, ("lat", "lon"), band_perm(lats, lons, step))
    other = lax.ppermute(theta, "lon", [(t, t ^ (lons // 2)) for t in range(lons)])
    theta4 = jnp.tile(jnp.where(turn[0] == 1, other, theta), (1, ENS))

    rest = (norm_gain[:, None], w_in, b_in[None, :], w_out)
    packed_low = pack(turn, fields, 0)
    low = swap(packed_low)
    coef_low, coef = coefs(
        row_start, row_count, (lat * ROWS).reshape(1), kernel, onward, packed_low
    )
    high = swap(pack(turn, fields, 1, coef, theta4, rest[0], rest[2]))
    after = shift(low, -1)
    share = low_share(low, onward, coef_low, theta4)
    high, share = lax.optimization_barrier((high, share))
    before = shift(high, 1)
    (conv_high,) = conv(me, coef, 1, share, high, after, theta4, onward, back, False)
    conv_high = swap(conv_high)
    pieces = conv(me, coef, 0, share, high, before, theta4, onward, back, True)
    conv_low = [pieces[0]] + [
        lax.ppermute(pieces[k], "lon", [(t, t ^ k) for t in range(lons)]) for k in range(1, lons)
    ]
    out = mlp(me, turn, [conv_high], fields, 1, *rest)
    return mlp(me, turn, conv_low, fields, 0, *rest, before=out)


def solution(mesh):
    placed = (
        P(None, "lat", "lon", None),
        P("lat", None, None, None),
        P(None, "lon"),
        P("lat"),
        P("lat"),
        P(),
        P(),
        P(),
        P(),
    )
    return jax.shard_map(
        shards, mesh=mesh, in_specs=placed, out_specs=P(None, "lat", "lon", None), check_vma=False
    )
```

```python
import functools

import jax
import jax.numpy as jnp
import ml_dtypes
import numpy as np
from jax import lax
from jax.experimental import pallas as pl
from jax.experimental.pallas import tpu as pltpu
from jax.sharding import PartitionSpec as P

BF16 = jnp.bfloat16
F32 = jnp.float32

LON_DEV = 8
ROWS = 8
HALF = 4
ENS = 4
CHUNK = 64
CHAN = 640
CH = 80
COLS = ENS * CH
NLON = 512
SLOTS = 9
KB = 3
FB = 16
FS = 16
BAND = HALF * 2 * FS
WIN = 12
PTS = ENS * HALF * CHUNK
HID = 1280
MID = CHAN // 2
LIMIT = 58 * 1024 * 1024
GROUP = 2
ANY = pl.BlockSpec(memory_space=pl.ANY)
SMEM = pl.BlockSpec(memory_space=pltpu.SMEM)
VMEM = pl.BlockSpec(memory_space=pltpu.VMEM)


def tables():
    point = np.arange(NLON)
    freq = np.arange(NLON // 2)
    angle = 2.0 * np.pi * ((freq[:, None] * point[None, :]) % NLON) / NLON
    re, im = np.cos(angle), -np.sin(angle)
    im[0] = np.cos(np.pi * point)
    weight = np.full((NLON // 2, 1), 2.0 / NLON)
    weight[0] = 1.0 / NLON
    onward = np.stack([re.reshape(FB, FS, NLON), im.reshape(FB, FS, NLON)], axis=1)
    back = np.stack(
        [(re * weight).reshape(FB, FS, NLON), (im * weight).reshape(FB, FS, NLON)], axis=1
    )
    return (
        onward.reshape(NLON, NLON).astype(ml_dtypes.bfloat16),
        back.reshape(NLON, NLON).astype(ml_dtypes.bfloat16),
    )


def params(*semantics):
    return pltpu.CompilerParams(vmem_limit_bytes=LIMIT, dimension_semantics=semantics)


def near(value):
    return pltpu.with_memory_space_constraint(value, pltpu.VMEM)


def block_of(index):
    return pl.ds(pl.multiple_of(index * CH, CH), CH)


def cost(flops, nbytes):
    return pl.CostEstimate(flops=int(flops), bytes_accessed=int(nbytes), transcendentals=0)


def pack_kernel(half, turn_ref, x_ref, *rest):
    o_ref, x_buf, o_buf, x_sem, o_sem = rest[-5:]
    wide = HALF * CHUNK
    copies = [
        pltpu.make_async_copy(x_ref.at[e, pl.ds(half * HALF, HALF)], x_buf.at[e], x_sem.at[e])
        for e in range(ENS)
    ]
    for c in copies:
        c.start()
    at = pl.multiple_of(turn_ref[0] * MID, MID)
    outs = []
    for e in range(ENS):
        copies[e].wait()
        x = x_buf[e].reshape(wide, CHAN).T
        lanes = slice(e * wide, (e + 1) * wide)
        o_buf[pl.ds(at, MID), lanes] = x[:MID]
        o_buf[pl.ds(MID - at, MID), lanes] = x[MID:]
        outs.append(pltpu.make_async_copy(o_buf.at[:, lanes], o_ref.at[:, lanes], o_sem.at[e]))
        outs[e].start()
    for c in outs:
        c.wait()


def pack(turn, fields, half, *after):
    return pl.pallas_call(
        functools.partial(pack_kernel, half),
        in_specs=[pl.BlockSpec(memory_space=pltpu.SMEM)] + [ANY] * (1 + len(after)),
        out_specs=ANY,
        out_shape=jax.ShapeDtypeStruct((CHAN, PTS), BF16),
        scratch_shapes=[
            pltpu.VMEM((ENS, HALF, CHUNK, CHAN), BF16),
            pltpu.VMEM((CHAN, PTS), BF16),
            pltpu.SemaphoreType.DMA((ENS,)),
            pltpu.SemaphoreType.DMA((ENS,)),
        ],
        compiler_params=params(),
        cost_estimate=cost(0, 4 * CHAN * PTS),
        name="pack",
    )(turn, fields, *after)


def dft_rows(x_ref, w, o_ref, at):
    for pair in range(2):
        rows = [[], []]
        for e in range(ENS):
            parts = [[], []]
            base = (e * 2 + pair) * 128
            for d in range(LON_DEV):
                tile = x_ref[d * CH : (d + 1) * CH, base : base + 128]
                parts[0].append(tile[:, :CHUNK])
                parts[1].append(tile[:, CHUNK:])
            for r in range(2):
                rows[r].append(jnp.concatenate(parts[r], axis=1))
        for r in range(2):
            x = jnp.concatenate(rows[r], axis=0)
            s = lax.dot_general(w, x, (((1,), (1,)), ((), ())), preferred_element_type=F32)
            row = at + (pair * 2 + r) * 2 * FS
            o_ref[:, row : row + 2 * FS, :] = s.astype(BF16).reshape(FB, 2 * FS, COLS)


def coef_kernel(start_ref, count_ref, first_ref, k_ref, w_ref, *rest):
    low_ref, rest_ref = rest[-2:]
    half = pl.program_id(0)
    kern = k_ref[...].astype(BF16)
    hat = lax.dot_general(w_ref[...], kern, (((1,), (1,)), ((), ())), preferred_element_type=F32)
    hat = hat.astype(BF16).reshape(FB, 2, FS, SLOTS * KB * HALF)
    hat_re = hat[:, 0].reshape(FB * FS, SLOTS * KB * HALF)
    hat_im = hat[:, 1].reshape(FB * FS, SLOTS * KB * HALF)
    lanes = WIN * 2 * FS
    taps = SLOTS * KB * HALF
    tap = lax.broadcasted_iota(jnp.int32, (taps, lanes), 0)
    window = lax.broadcasted_iota(jnp.int32, (taps, lanes), 1) // (2 * FS)
    window = jnp.where((half == 0) & (window < 2 * HALF), window ^ HALF, window)
    lane = lax.broadcasted_iota(jnp.int32, (FB * FS, lanes), 1)
    freq = lax.broadcasted_iota(jnp.int32, (FB * FS, lanes), 0)
    same = (lane % FS) == (freq % FS)
    imag = (lane // FS) % 2 == 1
    zero = freq == 0
    for i in range(HALF):
        row = half * HALF + i
        offset = start_ref[row] - (first_ref[0] + (half - 1) * HALF)
        slot = window - offset
        live = (slot >= 0) & (slot < count_ref[row])
        for k in range(KB):
            pick = (live & (tap == (i * SLOTS + slot) * KB + k)).astype(F32).astype(BF16)
            re = jnp.dot(hat_re, pick, preferred_element_type=F32)
            im = jnp.dot(hat_im, pick, preferred_element_type=F32)
            top = jnp.where(imag, jnp.where(zero, 0.0, -im), re)
            low = jnp.where(imag, jnp.where(zero, im, re), jnp.where(zero, 0.0, im))
            top = jnp.where(same, top, 0.0).astype(BF16).reshape(FB, FS, lanes)
            low = jnp.where(same, low, 0.0).astype(BF16).reshape(FB, FS, lanes)
            at = (i * KB + k) * 2 * FS
            low_ref[0, :, at : at + FS, :] = top[:, :, :BAND]
            rest_ref[0, :, at : at + FS, :] = top[:, :, BAND:]
            low_ref[0, :, at + FS : at + 2 * FS, :] = low[:, :, :BAND]
            rest_ref[0, :, at + FS : at + 2 * FS, :] = low[:, :, BAND:]


def coefs(row_start, row_count, first, kernel, onward, *after):
    smem = pl.BlockSpec(memory_space=pltpu.SMEM)
    taps = HALF * SLOTS * KB
    size = HALF * KB * 2 * FS
    return pl.pallas_call(
        coef_kernel,
        grid=(2,),
        in_specs=[
            smem,
            smem,
            smem,
            pl.BlockSpec((None, taps, NLON), lambda h: (h, 0, 0)),
            pl.BlockSpec((NLON, NLON), lambda h: (0, 0)),
        ]
        + [pl.BlockSpec(memory_space=pl.ANY)] * len(after),
        out_specs=[pl.BlockSpec((1, FB, size, n), lambda h: (h, 0, 0, 0)) for n in (BAND, 2 * BAND)],
        out_shape=[jax.ShapeDtypeStruct((2, FB, size, n), BF16) for n in (BAND, 2 * BAND)],
        compiler_params=params("arbitrary"),
        cost_estimate=cost(8e9, 1e7),
        name="coefs",
    )(row_start, row_count, first, kernel.reshape(2, taps, NLON), onward, *after)


def combine(p, theta):
    rows = []
    for i in range(HALF):
        total = None
        for k in range(KB):
            at = (i * KB + k) * 2 * FS
            term = p[at : at + 2 * FS, :] * theta[k]
            total = term if total is None else total + term
        rows.append(total)
    return rows


def low_kernel(x_ref, w_ref, g_ref, theta_ref, o_ref, s_buf):
    @pl.when(pl.program_id(0) == 0)
    def _():
        dft_rows(x_ref, w_ref[...], s_buf, 0)

    theta = [theta_ref[k : k + 1, :] for k in range(KB)]
    for block in range(FB):
        p = jnp.dot(g_ref[0, block], s_buf[block], preferred_element_type=F32)
        for i, row in enumerate(combine(p, theta)):
            o_ref[0, i, block * 2 * FS : (block + 1) * 2 * FS, :] = row


def low_share(received, onward, coef_low, theta):
    whole = lambda *shape: pl.BlockSpec(shape, lambda h: (0,) * len(shape))
    return pl.pallas_call(
        low_kernel,
        grid=(2,),
        in_specs=[
            whole(CHAN, PTS),
            whole(NLON, NLON),
            pl.BlockSpec((1, FB, HALF * KB * 2 * FS, BAND), lambda h: (h, 0, 0, 0)),
            whole(KB, COLS),
        ],
        out_specs=pl.BlockSpec((1, HALF, NLON, COLS), lambda h: (h, 0, 0, 0)),
        out_shape=jax.ShapeDtypeStruct((2, HALF, NLON, COLS), F32),
        scratch_shapes=[pltpu.VMEM((FB, BAND, COLS), BF16)],
        compiler_params=params("arbitrary"),
        cost_estimate=cost(2e9, 8e6),
        name="low",
    )(received, onward, coef_low, theta)


STEP = 4
STEPS = FB // STEP


def conv_kernel(
    half, me_ref, g_ref, low_ref, high_ref, halo_ref, theta_ref, w_ref, back_ref, *rest
):
    count = len(rest) - 11
    pieces, rest = rest[:count], rest[count:]
    o_buf, g_buf, s_buf, l_buf, x_buf, w_buf, t_buf, g_sem, l_sem, w_sem, o_sem = rest
    halo_at, high_at = (BAND, 0) if half else (0, BAND)
    moves = [(w_ref, w_buf.at[0]), (halo_ref, x_buf.at[1]), (back_ref, w_buf.at[1])]
    moves += [] if half else [(high_ref, x_buf.at[0])]
    ws = [pltpu.make_async_copy(ref, to, w_sem.at[n]) for n, (ref, to) in enumerate(moves)]
    gs, lows = [], []
    for s in range(STEPS):
        part = pl.ds(s * STEP, STEP)
        rows = pl.ds(s * STEP * 2 * FS, STEP * 2 * FS)
        gs.append(pltpu.make_async_copy(g_ref.at[half, part], g_buf.at[part], g_sem.at[s]))
        lows.append(pltpu.make_async_copy(low_ref.at[half, :, rows], l_buf.at[:, rows], l_sem.at[s]))
    for c in ws[:1] + ws[3:] + ws[1:2]:
        c.start()
    for s in range(STEPS):
        gs[s].start()
        lows[s].start()
    ws[2].start()
    for c in ws[:1] + ws[3:]:
        c.wait()
    dft_rows(high_ref if half else x_buf.at[0], w_buf[0], s_buf, high_at)
    ws[1].wait()
    dft_rows(x_buf.at[1], w_buf[0], s_buf, halo_at)
    theta = [theta_ref[k : k + 1, :] for k in range(KB)]
    for step in range(STEPS):
        gs[step].wait()
        lows[step].wait()
        for block in range(step * STEP, (step + 1) * STEP):
            p = jnp.dot(g_buf[block], s_buf[block], preferred_element_type=F32)
            rows = slice(block * 2 * FS, (block + 1) * 2 * FS)
            for i, row in enumerate(combine(p, theta)):
                t_buf[i, rows, :] = (row + l_buf[i, rows, :]).astype(BF16)
    ws[2].wait()
    outs = []
    for pair in range(2):
        y = [
            lax.dot_general(
                t_buf[pair * 2 + r],
                w_buf[1],
                (((0,), (0,)), ((), ())),
                preferred_element_type=F32,
            ).astype(BF16)
            for r in range(2)
        ]
        for e in range(ENS):
            base = (e * 2 + pair) * 128
            for d in range(LON_DEV):
                o_buf[d * CH : (d + 1) * CH, base : base + 128] = jnp.concatenate(
                    [v[e * CH : (e + 1) * CH, d * CHUNK : (d + 1) * CHUNK] for v in y], axis=1
                )
            if count == 1:
                lanes = slice(base, base + 128)
                outs.append(
                    pltpu.make_async_copy(
                        o_buf.at[:, lanes], pieces[0].at[:, lanes], o_sem.at[pair * ENS + e]
                    )
                )
                outs[-1].start()
    if count > 1:
        outs = [
            pltpu.make_async_copy(o_buf.at[block_of(me_ref[0] ^ k)], piece, o_sem.at[k])
            for k, piece in enumerate(pieces)
        ]
        for c in outs:
            c.start()
    for c in outs:
        c.wait()


def conv(me, coef, half, low, high, halo, theta, onward, back, split):
    size = HALF * KB * 2 * FS
    sems = pltpu.SemaphoreType.DMA
    shape = (CH, PTS) if split else (CHAN, PTS)
    count = LON_DEV if split else 1
    return pl.pallas_call(
        functools.partial(conv_kernel, half),
        in_specs=[SMEM, ANY, ANY, VMEM if half else ANY, ANY, VMEM, ANY, ANY],
        out_specs=[ANY] * count,
        out_shape=[jax.ShapeDtypeStruct(shape, BF16)] * count,
        scratch_shapes=[
            pltpu.VMEM((CHAN, PTS), BF16),
            pltpu.VMEM((FB, size, 2 * BAND), BF16),
            pltpu.VMEM((FB, 2 * BAND, COLS), BF16),
            pltpu.VMEM((HALF, NLON, COLS), F32),
            pltpu.VMEM((2, CHAN, PTS), BF16),
            pltpu.VMEM((2, NLON, NLON), BF16),
            pltpu.VMEM((HALF, NLON, COLS), BF16),
            sems((STEPS,)),
            sems((STEPS,)),
            sems((4,)),
            sems((LON_DEV,)),
        ],
        compiler_params=params(),
        cost_estimate=cost(6e9, 1.2e7),
        name="conv",
    )(me, coef, low, near(high) if half else high, halo, theta, onward, back)


def mlp_kernel(half, count, me_ref, turn_ref, *refs):
    pieces, refs = refs[:count], refs[count:]
    x_ref, gain_ref, w_in_ref, b_in_ref, w_out_ref, *rest = refs
    o_ref, y_buf, x_buf, w_in_buf, w_out_buf, o_buf, x_sem, w_sem, o_sem = rest[-9:]
    turned_by = turn_ref[0] * (LON_DEV // 2)
    wide = HALF * CHUNK
    rows = pl.ds(half * HALF, HALF)
    first = pltpu.make_async_copy(w_in_ref, w_in_buf, w_sem.at[0])
    second = pltpu.make_async_copy(w_out_ref, w_out_buf, w_sem.at[1])
    xs = [
        pltpu.make_async_copy(x_ref.at[e, rows], x_buf.at[e], x_sem.at[e]) for e in range(ENS)
    ]
    for c in [first, second, *xs]:
        c.start()
    if count > 1:
        for k, piece in enumerate(pieces):
            y_buf[block_of(me_ref[0] ^ k ^ turned_by), :] = piece[...]
    at = pl.multiple_of(turn_ref[0] * MID, MID)
    outs = []
    for part in range(ENS // GROUP):
        lanes = slice(part * GROUP * wide, (part + 1) * GROUP * wide)
        if count > 1:
            values = y_buf[:, lanes].astype(F32)
        else:
            y_ref = pieces[0]
            values = jnp.concatenate(
                [y_ref[pl.ds(at, MID), lanes], y_ref[pl.ds(MID - at, MID), lanes]], axis=0
            ).astype(F32)
        mean = jnp.mean(values, axis=0, keepdims=True)
        away = values - mean
        var = jnp.mean(away * away, axis=0, keepdims=True)
        normed = (away * lax.rsqrt(var + 1e-5) * gain_ref[...]).astype(BF16).T
        if part == 0:
            first.wait()
        hidden = jnp.dot(normed, w_in_buf[...], preferred_element_type=F32) + b_in_ref[...]
        hidden = (0.5 * hidden * (1.0 + lax.erf(hidden * np.float32(0.5**0.5)))).astype(BF16)
        if part == 0:
            second.wait()
        branch = jnp.dot(hidden, w_out_buf[...], preferred_element_type=F32)
        for g in range(GROUP):
            e = part * GROUP + g
            xs[e].wait()
            x = x_buf[e].reshape(wide, CHAN).astype(F32)
            o_buf[e] = (
                (x + branch[g * wide : (g + 1) * wide]).astype(BF16).reshape(HALF, CHUNK, CHAN)
            )
            outs.append(pltpu.make_async_copy(o_buf.at[e], o_ref.at[e, rows], o_sem.at[e]))
            outs[e].start()
    for c in outs:
        c.wait()


def mlp(me, turn, ys, fields, half, gain, w_in, b_in, w_out, before=None):
    extra = () if before is None else (before,)
    count = len(ys)
    points = (ENS, HALF, CHUNK, CHAN)
    sems = pltpu.SemaphoreType.DMA
    return pl.pallas_call(
        functools.partial(mlp_kernel, half, count),
        in_specs=[SMEM, SMEM]
        + [VMEM] * count
        + [ANY, VMEM, ANY, VMEM, ANY]
        + [ANY] * len(extra),
        out_specs=ANY,
        out_shape=jax.ShapeDtypeStruct((ENS, ROWS, CHUNK, CHAN), BF16),
        input_output_aliases={count + 7: 0} if extra else {},
        scratch_shapes=[
            pltpu.VMEM((CHAN, PTS) if count > 1 else (16, 128), BF16),
            pltpu.VMEM(points, BF16),
            pltpu.VMEM((CHAN, HID), BF16),
            pltpu.VMEM((HID, CHAN), BF16),
            pltpu.VMEM(points, BF16),
            sems((ENS,)),
            sems((2,)),
            sems((ENS,)),
        ],
        compiler_params=params(),
        cost_estimate=cost(4 * PTS * CHAN * HID, 1.2e7),
        name="mlp",
    )(me, turn, *(near(y) for y in ys), fields, gain, w_in, b_in, w_out, *extra)


def turned(lat):
    return (lat // 2) % 2


def band_perm(lats, lons, step):
    pairs = []
    for lat in range(lats):
        if 0 <= lat + step < lats:
            cross = (turned(lat) ^ turned(lat + step)) * (lons // 2)
            pairs += [(lat * lons + t, (lat + step) * lons + (t ^ cross)) for t in range(lons)]
    return pairs


def shards(fields, kernel, theta, row_start, row_count, norm_gain, w_in, b_in, w_out):
    onward, back = (jnp.asarray(t) for t in tables())
    lats, lons = lax.axis_size("lat"), lax.axis_size("lon")
    lat = lax.axis_index("lat").astype(jnp.int32)
    turn = turned(lat).reshape(1)
    me = lax.axis_index("lon").astype(jnp.int32).reshape(1)
    swap = functools.partial(
        lax.all_to_all, axis_name="lon", split_axis=0, concat_axis=0, tiled=True
    )
    shift = lambda v, step: lax.ppermute(v, ("lat", "lon"), band_perm(lats, lons, step))
    other = lax.ppermute(theta, "lon", [(t, t ^ (lons // 2)) for t in range(lons)])
    theta4 = jnp.tile(jnp.where(turn[0] == 1, other, theta), (1, ENS))

    rest = (norm_gain[:, None], w_in, b_in[None, :], w_out)
    packed_low = pack(turn, fields, 0)
    low = swap(packed_low)
    coef_low, coef = coefs(
        row_start, row_count, (lat * ROWS).reshape(1), kernel, onward, packed_low
    )
    high = swap(pack(turn, fields, 1, coef, theta4, rest[0], rest[2]))
    after = shift(low, -1)
    share = low_share(low, onward, coef_low, theta4)
    high, share = lax.optimization_barrier((high, share))
    before = shift(high, 1)
    (conv_high,) = conv(me, coef, 1, share, high, after, theta4, onward, back, False)
    conv_high = swap(conv_high)
    pieces = conv(me, coef, 0, share, high, before, theta4, onward, back, True)
    conv_low = [pieces[0]] + [
        lax.ppermute(pieces[k], "lon", [(t, t ^ k) for t in range(lons)]) for k in range(1, lons)
    ]
    out = mlp(me, turn, [conv_high], fields, 1, *rest)
    return mlp(me, turn, conv_low, fields, 0, *rest, before=out)


def solution(mesh):
    placed = (
        P(None, "lat", "lon", None),
        P("lat", None, None, None),
        P(None, "lon"),
        P("lat"),
        P("lat"),
        P(),
        P(),
        P(),
        P(),
    )
    return jax.shard_map(
        shards, mesh=mesh, in_specs=placed, out_specs=P(None, "lat", "lon", None), check_vma=False
    )
```

```python
import functools

import jax
import jax.numpy as jnp
import ml_dtypes
import numpy as np
from jax import lax
from jax.experimental import pallas as pl
from jax.experimental.pallas import tpu as pltpu
from jax.sharding import PartitionSpec as P

BF16 = jnp.bfloat16
F32 = jnp.float32

LON_DEV = 8
ROWS = 8
HALF = 4
ENS = 4
CHUNK = 64
CHAN = 640
CH = 80
COLS = ENS * CH
NLON = 512
SLOTS = 9
KB = 3
FB = 16
FS = 16
BAND = HALF * 2 * FS
WIN = 12
PTS = ENS * HALF * CHUNK
HID = 1280
MID = CHAN // 2
LIMIT = 58 * 1024 * 1024
GROUP = 4
ANY = pl.BlockSpec(memory_space=pl.ANY)
SMEM = pl.BlockSpec(memory_space=pltpu.SMEM)
VMEM = pl.BlockSpec(memory_space=pltpu.VMEM)


def tables():
    point = np.arange(NLON)
    freq = np.arange(NLON // 2)
    angle = 2.0 * np.pi * ((freq[:, None] * point[None, :]) % NLON) / NLON
    re, im = np.cos(angle), -np.sin(angle)
    im[0] = np.cos(np.pi * point)
    weight = np.full((NLON // 2, 1), 2.0 / NLON)
    weight[0] = 1.0 / NLON
    onward = np.stack([re.reshape(FB, FS, NLON), im.reshape(FB, FS, NLON)], axis=1)
    back = np.stack(
        [(re * weight).reshape(FB, FS, NLON), (im * weight).reshape(FB, FS, NLON)], axis=1
    )
    return (
        onward.reshape(NLON, NLON).astype(ml_dtypes.bfloat16),
        back.reshape(NLON, NLON).astype(ml_dtypes.bfloat16),
    )


def params(*semantics):
    return pltpu.CompilerParams(vmem_limit_bytes=LIMIT, dimension_semantics=semantics)


def near(value):
    return pltpu.with_memory_space_constraint(value, pltpu.VMEM)


def block_of(index):
    return pl.ds(pl.multiple_of(index * CH, CH), CH)


def cost(flops, nbytes):
    return pl.CostEstimate(flops=int(flops), bytes_accessed=int(nbytes), transcendentals=0)


def pack_kernel(half, turn_ref, x_ref, *rest):
    o_ref, x_buf, o_buf, x_sem, o_sem = rest[-5:]
    wide = HALF * CHUNK
    copies = [
        pltpu.make_async_copy(x_ref.at[e, pl.ds(half * HALF, HALF)], x_buf.at[e], x_sem.at[e])
        for e in range(ENS)
    ]
    for c in copies:
        c.start()
    at = pl.multiple_of(turn_ref[0] * MID, MID)
    outs = []
    for e in range(ENS):
        copies[e].wait()
        x = x_buf[e].reshape(wide, CHAN).T
        lanes = slice(e * wide, (e + 1) * wide)
        o_buf[pl.ds(at, MID), lanes] = x[:MID]
        o_buf[pl.ds(MID - at, MID), lanes] = x[MID:]
        outs.append(pltpu.make_async_copy(o_buf.at[:, lanes], o_ref.at[:, lanes], o_sem.at[e]))
        outs[e].start()
    for c in outs:
        c.wait()


def pack(turn, fields, half, *after):
    return pl.pallas_call(
        functools.partial(pack_kernel, half),
        in_specs=[pl.BlockSpec(memory_space=pltpu.SMEM)] + [ANY] * (1 + len(after)),
        out_specs=ANY,
        out_shape=jax.ShapeDtypeStruct((CHAN, PTS), BF16),
        scratch_shapes=[
            pltpu.VMEM((ENS, HALF, CHUNK, CHAN), BF16),
            pltpu.VMEM((CHAN, PTS), BF16),
            pltpu.SemaphoreType.DMA((ENS,)),
            pltpu.SemaphoreType.DMA((ENS,)),
        ],
        compiler_params=params(),
        cost_estimate=cost(0, 4 * CHAN * PTS),
        name="pack",
    )(turn, fields, *after)


def dft_rows(x_ref, w, o_ref, at):
    for pair in range(2):
        rows = [[], []]
        for e in range(ENS):
            parts = [[], []]
            base = (e * 2 + pair) * 128
            for d in range(LON_DEV):
                tile = x_ref[d * CH : (d + 1) * CH, base : base + 128]
                parts[0].append(tile[:, :CHUNK])
                parts[1].append(tile[:, CHUNK:])
            for r in range(2):
                rows[r].append(jnp.concatenate(parts[r], axis=1))
        for r in range(2):
            x = jnp.concatenate(rows[r], axis=0)
            s = lax.dot_general(w, x, (((1,), (1,)), ((), ())), preferred_element_type=F32)
            row = at + (pair * 2 + r) * 2 * FS
            o_ref[:, row : row + 2 * FS, :] = s.astype(BF16).reshape(FB, 2 * FS, COLS)


def coef_kernel(start_ref, count_ref, first_ref, k_ref, w_ref, *rest):
    low_ref, rest_ref = rest[-2:]
    half = pl.program_id(0)
    kern = k_ref[...].astype(BF16)
    hat = lax.dot_general(w_ref[...], kern, (((1,), (1,)), ((), ())), preferred_element_type=F32)
    hat = hat.astype(BF16).reshape(FB, 2, FS, SLOTS * KB * HALF)
    hat_re = hat[:, 0].reshape(FB * FS, SLOTS * KB * HALF)
    hat_im = hat[:, 1].reshape(FB * FS, SLOTS * KB * HALF)
    lanes = WIN * 2 * FS
    taps = SLOTS * KB * HALF
    tap = lax.broadcasted_iota(jnp.int32, (taps, lanes), 0)
    window = lax.broadcasted_iota(jnp.int32, (taps, lanes), 1) // (2 * FS)
    window = jnp.where((half == 0) & (window < 2 * HALF), window ^ HALF, window)
    lane = lax.broadcasted_iota(jnp.int32, (FB * FS, lanes), 1)
    freq = lax.broadcasted_iota(jnp.int32, (FB * FS, lanes), 0)
    same = (lane % FS) == (freq % FS)
    imag = (lane // FS) % 2 == 1
    zero = freq == 0
    for i in range(HALF):
        row = half * HALF + i
        offset = start_ref[row] - (first_ref[0] + (half - 1) * HALF)
        slot = window - offset
        live = (slot >= 0) & (slot < count_ref[row])
        for k in range(KB):
            pick = (live & (tap == (i * SLOTS + slot) * KB + k)).astype(F32).astype(BF16)
            re = jnp.dot(hat_re, pick, preferred_element_type=F32)
            im = jnp.dot(hat_im, pick, preferred_element_type=F32)
            top = jnp.where(imag, jnp.where(zero, 0.0, -im), re)
            low = jnp.where(imag, jnp.where(zero, im, re), jnp.where(zero, 0.0, im))
            top = jnp.where(same, top, 0.0).astype(BF16).reshape(FB, FS, lanes)
            low = jnp.where(same, low, 0.0).astype(BF16).reshape(FB, FS, lanes)
            at = (i * KB + k) * 2 * FS
            low_ref[0, :, at : at + FS, :] = top[:, :, :BAND]
            rest_ref[0, :, at : at + FS, :] = top[:, :, BAND:]
            low_ref[0, :, at + FS : at + 2 * FS, :] = low[:, :, :BAND]
            rest_ref[0, :, at + FS : at + 2 * FS, :] = low[:, :, BAND:]


def coefs(row_start, row_count, first, kernel, onward, *after):
    smem = pl.BlockSpec(memory_space=pltpu.SMEM)
    taps = HALF * SLOTS * KB
    size = HALF * KB * 2 * FS
    return pl.pallas_call(
        coef_kernel,
        grid=(2,),
        in_specs=[
            smem,
            smem,
            smem,
            pl.BlockSpec((None, taps, NLON), lambda h: (h, 0, 0)),
            pl.BlockSpec((NLON, NLON), lambda h: (0, 0)),
        ]
        + [pl.BlockSpec(memory_space=pl.ANY)] * len(after),
        out_specs=[pl.BlockSpec((1, FB, size, n), lambda h: (h, 0, 0, 0)) for n in (BAND, 2 * BAND)],
        out_shape=[jax.ShapeDtypeStruct((2, FB, size, n), BF16) for n in (BAND, 2 * BAND)],
        compiler_params=params("arbitrary"),
        cost_estimate=cost(8e9, 1e7),
        name="coefs",
    )(row_start, row_count, first, kernel.reshape(2, taps, NLON), onward, *after)


def combine(p, theta):
    rows = []
    for i in range(HALF):
        total = None
        for k in range(KB):
            at = (i * KB + k) * 2 * FS
            term = p[at : at + 2 * FS, :] * theta[k]
            total = term if total is None else total + term
        rows.append(total)
    return rows


def low_kernel(x_ref, w_ref, g_ref, theta_ref, o_ref, s_buf):
    @pl.when(pl.program_id(0) == 0)
    def _():
        dft_rows(x_ref, w_ref[...], s_buf, 0)

    theta = [theta_ref[k : k + 1, :] for k in range(KB)]
    for block in range(FB):
        p = jnp.dot(g_ref[0, block], s_buf[block], preferred_element_type=F32)
        for i, row in enumerate(combine(p, theta)):
            o_ref[0, i, block * 2 * FS : (block + 1) * 2 * FS, :] = row


def low_share(received, onward, coef_low, theta):
    whole = lambda *shape: pl.BlockSpec(shape, lambda h: (0,) * len(shape))
    return pl.pallas_call(
        low_kernel,
        grid=(2,),
        in_specs=[
            whole(CHAN, PTS),
            whole(NLON, NLON),
            pl.BlockSpec((1, FB, HALF * KB * 2 * FS, BAND), lambda h: (h, 0, 0, 0)),
            whole(KB, COLS),
        ],
        out_specs=pl.BlockSpec((1, HALF, NLON, COLS), lambda h: (h, 0, 0, 0)),
        out_shape=jax.ShapeDtypeStruct((2, HALF, NLON, COLS), F32),
        scratch_shapes=[pltpu.VMEM((FB, BAND, COLS), BF16)],
        compiler_params=params("arbitrary"),
        cost_estimate=cost(2e9, 8e6),
        name="low",
    )(received, onward, coef_low, theta)


STEP = 4
STEPS = FB // STEP


def conv_kernel(
    half, me_ref, g_ref, low_ref, high_ref, halo_ref, theta_ref, w_ref, back_ref, *rest
):
    count = len(rest) - 11
    pieces, rest = rest[:count], rest[count:]
    o_buf, g_buf, s_buf, l_buf, x_buf, w_buf, t_buf, g_sem, l_sem, w_sem, o_sem = rest
    halo_at, high_at = (BAND, 0) if half else (0, BAND)
    moves = [(w_ref, w_buf.at[0]), (back_ref, w_buf.at[1])]
    ws = [pltpu.make_async_copy(ref, to, w_sem.at[n]) for n, (ref, to) in enumerate(moves)]
    gs, lows = [], []
    for s in range(STEPS):
        part = pl.ds(s * STEP, STEP)
        rows = pl.ds(s * STEP * 2 * FS, STEP * 2 * FS)
        gs.append(pltpu.make_async_copy(g_ref.at[half, part], g_buf.at[part], g_sem.at[s]))
        lows.append(pltpu.make_async_copy(low_ref.at[half, :, rows], l_buf.at[:, rows], l_sem.at[s]))
    for c in ws[:1] + ws[2:]:
        c.start()
    for s in range(STEPS):
        gs[s].start()
        lows[s].start()
    ws[1].start()
    for c in ws[:1] + ws[2:]:
        c.wait()
    dft_rows(high_ref, w_buf[0], s_buf, high_at)
    dft_rows(halo_ref, w_buf[0], s_buf, halo_at)
    theta = [theta_ref[k : k + 1, :] for k in range(KB)]
    for step in range(STEPS):
        gs[step].wait()
        lows[step].wait()
        for block in range(step * STEP, (step + 1) * STEP):
            p = jnp.dot(g_buf[block], s_buf[block], preferred_element_type=F32)
            rows = slice(block * 2 * FS, (block + 1) * 2 * FS)
            for i, row in enumerate(combine(p, theta)):
                t_buf[i, rows, :] = (row + l_buf[i, rows, :]).astype(BF16)
    ws[1].wait()
    outs = []
    for pair in range(2):
        y = [
            lax.dot_general(
                t_buf[pair * 2 + r],
                w_buf[1],
                (((0,), (0,)), ((), ())),
                preferred_element_type=F32,
            ).astype(BF16)
            for r in range(2)
        ]
        for e in range(ENS):
            base = (e * 2 + pair) * 128
            for d in range(LON_DEV):
                o_buf[d * CH : (d + 1) * CH, base : base + 128] = jnp.concatenate(
                    [v[e * CH : (e + 1) * CH, d * CHUNK : (d + 1) * CHUNK] for v in y], axis=1
                )
            if count == 1:
                lanes = slice(base, base + 128)
                outs.append(
                    pltpu.make_async_copy(
                        o_buf.at[:, lanes], pieces[0].at[:, lanes], o_sem.at[pair * ENS + e]
                    )
                )
                outs[-1].start()
    if count > 1:
        outs = [
            pltpu.make_async_copy(o_buf.at[block_of(me_ref[0] ^ k)], piece, o_sem.at[k])
            for k, piece in enumerate(pieces)
        ]
        for c in outs:
            c.start()
    for c in outs:
        c.wait()


def conv(me, coef, half, low, high, halo, theta, onward, back, split):
    size = HALF * KB * 2 * FS
    sems = pltpu.SemaphoreType.DMA
    shape = (CH, PTS) if split else (CHAN, PTS)
    count = LON_DEV if split else 1
    return pl.pallas_call(
        functools.partial(conv_kernel, half),
        in_specs=[SMEM, ANY, ANY] + [VMEM] * 2 + [VMEM, ANY, ANY],
        out_specs=[ANY] * count,
        out_shape=[jax.ShapeDtypeStruct(shape, BF16)] * count,
        scratch_shapes=[
            pltpu.VMEM((CHAN, PTS), BF16),
            pltpu.VMEM((FB, size, 2 * BAND), BF16),
            pltpu.VMEM((FB, 2 * BAND, COLS), BF16),
            pltpu.VMEM((HALF, NLON, COLS), F32),
            pltpu.VMEM((2, CHAN, PTS), BF16),
            pltpu.VMEM((2, NLON, NLON), BF16),
            pltpu.VMEM((HALF, NLON, COLS), BF16),
            sems((STEPS,)),
            sems((STEPS,)),
            sems((4,)),
            sems((LON_DEV,)),
        ],
        compiler_params=params(),
        cost_estimate=cost(6e9, 1.2e7),
        name="conv",
    )(me, coef, low, near(high), near(halo), theta, onward, back)


def mlp_kernel(half, count, me_ref, turn_ref, *refs):
    pieces, refs = refs[:count], refs[count:]
    x_ref, gain_ref, w_in_ref, b_in_ref, w_out_ref, *rest = refs
    o_ref, y_buf, x_buf, w_in_buf, w_out_buf, o_buf, x_sem, w_sem, o_sem = rest[-9:]
    turned_by = turn_ref[0] * (LON_DEV // 2)
    wide = HALF * CHUNK
    rows = pl.ds(half * HALF, HALF)
    first = pltpu.make_async_copy(w_in_ref, w_in_buf, w_sem.at[0])
    second = pltpu.make_async_copy(w_out_ref, w_out_buf, w_sem.at[1])
    xs = [
        pltpu.make_async_copy(x_ref.at[e, rows], x_buf.at[e], x_sem.at[e]) for e in range(ENS)
    ]
    for c in [first, second, *xs]:
        c.start()
    if count > 1:
        for k, piece in enumerate(pieces):
            y_buf[block_of(me_ref[0] ^ k ^ turned_by), :] = piece[...]
    at = pl.multiple_of(turn_ref[0] * MID, MID)
    outs = []
    for part in range(ENS // GROUP):
        lanes = slice(part * GROUP * wide, (part + 1) * GROUP * wide)
        if count > 1:
            values = y_buf[:, lanes].astype(F32)
        else:
            y_ref = pieces[0]
            values = jnp.concatenate(
                [y_ref[pl.ds(at, MID), lanes], y_ref[pl.ds(MID - at, MID), lanes]], axis=0
            ).astype(F32)
        mean = jnp.mean(values, axis=0, keepdims=True)
        away = values - mean
        var = jnp.mean(away * away, axis=0, keepdims=True)
        normed = (away * lax.rsqrt(var + 1e-5) * gain_ref[...]).astype(BF16).T
        if part == 0:
            first.wait()
        hidden = jnp.dot(normed, w_in_buf[...], preferred_element_type=F32) + b_in_ref[...]
        hidden = (0.5 * hidden * (1.0 + lax.erf(hidden * np.float32(0.5**0.5)))).astype(BF16)
        if part == 0:
            second.wait()
        branch = jnp.dot(hidden, w_out_buf[...], preferred_element_type=F32)
        for g in range(GROUP):
            e = part * GROUP + g
            xs[e].wait()
            x = x_buf[e].reshape(wide, CHAN).astype(F32)
            o_buf[e] = (
                (x + branch[g * wide : (g + 1) * wide]).astype(BF16).reshape(HALF, CHUNK, CHAN)
            )
            outs.append(pltpu.make_async_copy(o_buf.at[e], o_ref.at[e, rows], o_sem.at[e]))
            outs[e].start()
    for c in outs:
        c.wait()


def mlp(me, turn, ys, fields, half, gain, w_in, b_in, w_out, before=None):
    extra = () if before is None else (before,)
    count = len(ys)
    points = (ENS, HALF, CHUNK, CHAN)
    sems = pltpu.SemaphoreType.DMA
    return pl.pallas_call(
        functools.partial(mlp_kernel, half, count),
        in_specs=[SMEM, SMEM]
        + [VMEM] * count
        + [ANY, VMEM, ANY, VMEM, ANY]
        + [ANY] * len(extra),
        out_specs=ANY,
        out_shape=jax.ShapeDtypeStruct((ENS, ROWS, CHUNK, CHAN), BF16),
        input_output_aliases={count + 7: 0} if extra else {},
        scratch_shapes=[
            pltpu.VMEM((CHAN, PTS) if count > 1 else (16, 128), BF16),
            pltpu.VMEM(points, BF16),
            pltpu.VMEM((CHAN, HID), BF16),
            pltpu.VMEM((HID, CHAN), BF16),
            pltpu.VMEM(points, BF16),
            sems((ENS,)),
            sems((2,)),
            sems((ENS,)),
        ],
        compiler_params=params(),
        cost_estimate=cost(4 * PTS * CHAN * HID, 1.2e7),
        name="mlp",
    )(me, turn, *(near(y) for y in ys), fields, gain, w_in, b_in, w_out, *extra)


def turned(lat):
    return (lat // 2) % 2


def band_perm(lats, lons, step):
    pairs = []
    for lat in range(lats):
        if 0 <= lat + step < lats:
            cross = (turned(lat) ^ turned(lat + step)) * (lons // 2)
            pairs += [(lat * lons + t, (lat + step) * lons + (t ^ cross)) for t in range(lons)]
    return pairs


def shards(fields, kernel, theta, row_start, row_count, norm_gain, w_in, b_in, w_out):
    onward, back = (jnp.asarray(t) for t in tables())
    lats, lons = lax.axis_size("lat"), lax.axis_size("lon")
    lat = lax.axis_index("lat").astype(jnp.int32)
    turn = turned(lat).reshape(1)
    me = lax.axis_index("lon").astype(jnp.int32).reshape(1)
    swap = functools.partial(
        lax.all_to_all, axis_name="lon", split_axis=0, concat_axis=0, tiled=True
    )
    shift = lambda v, step: lax.ppermute(v, ("lat", "lon"), band_perm(lats, lons, step))
    other = lax.ppermute(theta, "lon", [(t, t ^ (lons // 2)) for t in range(lons)])
    theta4 = jnp.tile(jnp.where(turn[0] == 1, other, theta), (1, ENS))

    rest = (norm_gain[:, None], w_in, b_in[None, :], w_out)
    packed_low = pack(turn, fields, 0)
    low = swap(packed_low)
    coef_low, coef = coefs(
        row_start, row_count, (lat * ROWS).reshape(1), kernel, onward, packed_low
    )
    high = swap(pack(turn, fields, 1, coef, theta4, rest[0], rest[2]))
    after = shift(low, -1)
    share = low_share(low, onward, coef_low, theta4)
    high, share = lax.optimization_barrier((high, share))
    before = shift(high, 1)
    (conv_high,) = conv(me, coef, 1, share, high, after, theta4, onward, back, False)
    conv_high = swap(conv_high)
    pieces = conv(me, coef, 0, share, high, before, theta4, onward, back, True)
    conv_low = [pieces[0]] + [
        lax.ppermute(pieces[k], "lon", [(t, t ^ k) for t in range(lons)]) for k in range(1, lons)
    ]
    out = mlp(me, turn, [conv_high], fields, 1, *rest)
    return mlp(me, turn, conv_low, fields, 0, *rest, before=out)


def solution(mesh):
    placed = (
        P(None, "lat", "lon", None),
        P("lat", None, None, None),
        P(None, "lon"),
        P("lat"),
        P("lat"),
        P(),
        P(),
        P(),
        P(),
    )
    return jax.shard_map(
        shards, mesh=mesh, in_specs=placed, out_specs=P(None, "lat", "lon", None), check_vma=False
    )
```
